32 devices in a mesh: pipe: 4 (over x, core), ctx: 8 (over z, y).
Axes of the slice: x: 2, y: 2, z: 4, core: 2. Of those that a mesh axis runs over, the one named last changes fastest.
Arguments:
- queries: bfloat16 [2, 4, 1024, 2560], P(None, 'pipe', 'ctx'), may hold values from -80 to 80
- keys: bfloat16 [2, 4, 1024, 512], P(None, 'pipe', 'ctx'), may hold values from -25 to 25
- values: bfloat16 [2, 4, 1024, 512], P(None, 'pipe', 'ctx'), may hold values from -6 to 6
- grad_a: bfloat16 [4, 1024, 2560], P('pipe', 'ctx'), may hold values from -96 to 96
- grad_b: bfloat16 [4, 1024, 2560], P('pipe', 'ctx'), may hold values from -48 to 48
- imports: int32 [2, 4, 8, 8], P(None, 'pipe'), may hold values from 0 to 1, as said below
- block_ids: int32 [2, 4, 8], P(None, 'pipe'), may hold values from 0 to 7, each once within a row
Outputs:
- dq_a: bfloat16 [4, 1024, 2560], P('pipe', 'ctx')
- dq_b: bfloat16 [4, 1024, 2560], P('pipe', 'ctx')
- kv_grads: bfloat16 [2, 4, 1024, 1024], P(None, 'pipe', 'ctx')
The draws below stay inside these ranges and needn't reach their ends.
Inputs may be any that keep to these rules, and one draw needn't show every extreme that they name: Every file block sees itself and imports at most 7 other blocks; in each micro-batch and section some block imports exactly 7.
All inputs are finite; a program needn't handle non-finite values.
Results may differ from the reference program's by a relative error of at most 0.015.
Values may be sent and summed in bfloat16 or wider, within the bound.
No kernel may reach another device: no remote copies, remote signals or barrier semaphores. Data moves between devices by JAX's collectives and lax.ppermute only.
A program may use at most 64 MiB of HBM per device.

```python
import math
import jax
import jax.numpy as jnp
from jax import lax

QUERY_HEADS = 20
KEY_VALUE_HEADS = 4
HEAD_DIMENSION = 128
FILE_BLOCK_SIZE = 128
BPD = 1
MICRO_BATCHES = 2
FILE_BLOCKS = 8
MICRO_LENGTH = 1024
IMP = 7
N_PIPE = 4
N_CTX = 8


def pair_fields(key):
    base_key = jax.random.fold_in(key, 7)
    key_query, key_random_keys = jax.random.split(base_key, 2)
    query_part = jax.random.normal(key_query, (MICRO_BATCHES, N_PIPE, FILE_BLOCKS, FILE_BLOCK_SIZE, QUERY_HEADS, HEAD_DIMENSION), jnp.float32)
    key_portion = jax.random.normal(key_random_keys, (MICRO_BATCHES, N_PIPE, FILE_BLOCKS, FILE_BLOCK_SIZE, KEY_VALUE_HEADS, HEAD_DIMENSION), jnp.float32)
    return (query_part, key_portion)


def draw_queries(key, part):
    query_part, key_portion = pair_fields(key)
    return jnp.clip(query_part, -80.0, 80.0).reshape(MICRO_BATCHES, N_PIPE, MICRO_LENGTH, QUERY_HEADS * HEAD_DIMENSION).astype(jnp.bfloat16)


def draw_keys(key, part):
    query_part, key_portion = pair_fields(key)
    return jnp.clip(key_portion, -25.0, 25.0).reshape(MICRO_BATCHES, N_PIPE, MICRO_LENGTH, KEY_VALUE_HEADS * HEAD_DIMENSION).astype(jnp.bfloat16)


def draw_imports(key, part):
    base_key = jax.random.fold_in(key, 29)
    key_first, key_second, key_pick, key_rank = jax.random.split(base_key, 4)
    lead_shape = (MICRO_BATCHES, N_PIPE)
    first_draw = jax.random.randint(key_first, lead_shape + (FILE_BLOCKS,), 0, IMP + 1)
    second_draw = jax.random.randint(key_second, lead_shape + (FILE_BLOCKS,), 0, IMP + 1)
    counts = first_draw * second_draw // IMP
    chosen = jax.random.randint(key_pick, lead_shape + (1,), 0, FILE_BLOCKS)
    column = jnp.arange(FILE_BLOCKS, dtype=jnp.int32)
    counts = jnp.where(column[None, None, :] == chosen, IMP, counts)
    ranking = jax.random.randint(key_rank, lead_shape + (FILE_BLOCKS, FILE_BLOCKS), 0, 4096) * FILE_BLOCKS + column
    diagonal = column[:, None] == column[None, :]
    ranking = jnp.where(diagonal, 4096 * FILE_BLOCKS + FILE_BLOCKS, ranking)
    sort_order = jnp.argsort(ranking, axis=-1, stable=True)
    position = jnp.argsort(sort_order, axis=-1, stable=True)
    selected_entries = (position < counts[..., None]) | diagonal
    return selected_entries.astype(jnp.int32)


def shard_levels(rng, extent, shards, least, largest):
    gain, own = 1.0, jax.random.fold_in(rng, 6)
    for dim, blocks in shards:
        draws = jnp.exp(jax.random.uniform(jax.random.fold_in(own, dim), (blocks,), jnp.float32, least / len(shards), largest / len(shards)))
        gain = gain * jnp.repeat(draws, extent[dim] // blocks).reshape([-1 if axis == dim else 1 for axis in range(len(extent))])
    return gain


def bell_draw(key, extent, deviation, reach, cuts=(), kind=jnp.bfloat16):
    drawn = jax.random.normal(key, extent, jnp.float32) * deviation
    if len(cuts) > 0:
        drawn = shard_levels(key, extent, cuts, -0.22, 0.18) * drawn
    return jnp.clip(drawn, min=-reach, max=reach).astype(kind)


def setup_inputs(seed: int = 0) -> dict:
    seeds = jax.random.split(jax.random.key(seed), 8)
    queries = draw_queries(jax.random.fold_in(seeds[7], 71), 0)
    keys = draw_keys(jax.random.fold_in(seeds[7], 71), 0)
    values = bell_draw(seeds[2], (MICRO_BATCHES, N_PIPE, MICRO_LENGTH, KEY_VALUE_HEADS * HEAD_DIMENSION), 1.0, 6.0, ((1, 4), (2, 8)))
    grad_a = bell_draw(seeds[3], (N_PIPE, MICRO_LENGTH, QUERY_HEADS * HEAD_DIMENSION), 16.0, 96.0, ((0, 4), (1, 8)))
    grad_b = bell_draw(seeds[4], (N_PIPE, MICRO_LENGTH, QUERY_HEADS * HEAD_DIMENSION), 8.0, 48.0, ((0, 4), (1, 8)))
    imports = draw_imports(jax.random.fold_in(seeds[7], 71), 0)
    block_ids = jax.vmap(lambda own: jax.random.permutation(own, FILE_BLOCKS))(jax.random.split(seeds[6], MICRO_BATCHES * N_PIPE)).reshape((MICRO_BATCHES, N_PIPE, FILE_BLOCKS)).astype(jnp.int32)
    return dict(queries=queries, keys=keys, values=values, grad_a=grad_a, grad_b=grad_b, imports=imports, block_ids=block_ids)


negative_large = -1e+30

def lowered(values_in):
    return lax.optimization_barrier(values_in.astype(jnp.bfloat16)).astype(jnp.float32)

def slot_table(import_mask, block_order):
    onehot = (block_order[:, None] == jnp.arange(FILE_BLOCKS, dtype=jnp.int32)[None, :]).astype(jnp.float32)
    mapped = jnp.dot(onehot, import_mask.astype(jnp.float32), precision=lax.Precision.HIGHEST)
    return jnp.dot(mapped, onehot.T, precision=lax.Precision.HIGHEST)

def block_grads(query_row_tensor, gradient_rows, selected_keys, selected_values, key_slots, key_live, slot_index, softmax_scale):
    query_group_width = QUERY_HEADS // KEY_VALUE_HEADS
    selected_entries = key_slots.shape[0]
    query_head_tensor = query_row_tensor.astype(jnp.float32).reshape(FILE_BLOCK_SIZE, KEY_VALUE_HEADS, query_group_width, HEAD_DIMENSION)
    gradient_heads = gradient_rows.astype(jnp.float32).reshape(FILE_BLOCK_SIZE, KEY_VALUE_HEADS, query_group_width, HEAD_DIMENSION)
    flattened_keys = selected_keys.astype(jnp.float32).reshape(selected_entries * FILE_BLOCK_SIZE, KEY_VALUE_HEADS, HEAD_DIMENSION)
    flattened_values = selected_values.astype(jnp.float32).reshape(selected_entries * FILE_BLOCK_SIZE, KEY_VALUE_HEADS, HEAD_DIMENSION)
    column_slot = jnp.repeat(key_slots, FILE_BLOCK_SIZE)
    column_place = jnp.tile(jnp.arange(FILE_BLOCK_SIZE, dtype=jnp.int32), selected_entries)
    column_live = jnp.repeat(key_live, FILE_BLOCK_SIZE)
    row_place = jnp.arange(FILE_BLOCK_SIZE, dtype=jnp.int32)
    allowed = column_live[None, :] & ((column_slot != slot_index)[None, :] | (column_place[None, :] <= row_place[:, None]))
    scores = jnp.einsum('rhgd,khd->hgrk', query_head_tensor, flattened_keys) * softmax_scale
    masked = jnp.where(allowed, scores, negative_large)
    row_max = lax.optimization_barrier(jnp.max(masked, axis=-1))
    expo = jnp.where(allowed, jnp.exp(masked - row_max[..., None]), 0.0)
    row_sum = lax.optimization_barrier(jnp.sum(expo, axis=-1))
    weighted = jnp.einsum('hgrk,khd->rhgd', lowered(expo), flattened_values)
    attended = weighted / jnp.transpose(row_sum, (2, 0, 1))[..., None]
    log_total = row_max + jnp.log(row_sum)
    delta = jnp.transpose(lax.optimization_barrier(jnp.sum(gradient_heads * attended, axis=-1)), (1, 2, 0))
    probs = jnp.where(allowed, jnp.exp(jnp.where(allowed, scores - log_total[..., None], negative_large)), 0.0)
    value_gradient = jnp.einsum('hgrk,rhgd->khd', lowered(probs), gradient_heads)
    prob_grad = jnp.einsum('rhgd,khd->hgrk', gradient_heads, flattened_values)
    score_grad = lowered(probs * (prob_grad - delta[..., None]))
    q_grad = jnp.einsum('hgrk,khd->rhgd', score_grad, flattened_keys) * softmax_scale
    key_gradient = jnp.einsum('hgrk,rhgd->khd', score_grad, query_head_tensor) * softmax_scale
    key_value_block = jnp.concatenate([key_gradient.reshape(selected_entries * FILE_BLOCK_SIZE, KEY_VALUE_HEADS * HEAD_DIMENSION), value_gradient.reshape(selected_entries * FILE_BLOCK_SIZE, KEY_VALUE_HEADS * HEAD_DIMENSION)], axis=1)
    return (q_grad.reshape(FILE_BLOCK_SIZE, QUERY_HEADS * HEAD_DIMENSION), key_value_block)

def section_micro(query_all, every_key, every_value, incoming_gradient, import_mask, block_order, softmax_scale):
    slot_mask = slot_table(import_mask, block_order)
    column_counts = 2 * KEY_VALUE_HEADS * HEAD_DIMENSION
    key_block_list = every_key.reshape(FILE_BLOCKS, FILE_BLOCK_SIZE, KEY_VALUE_HEADS, HEAD_DIMENSION)
    value_block_list = every_value.reshape(FILE_BLOCKS, FILE_BLOCK_SIZE, KEY_VALUE_HEADS, HEAD_DIMENSION)

    def device_turn(carried, device):
        partial_sum = jnp.zeros((FILE_BLOCKS, FILE_BLOCK_SIZE, column_counts), jnp.float32)
        q_parts = []
        for local_index in range(BPD):
            slot_index = (device * BPD + local_index).astype(jnp.int32)
            query_row_tensor = lax.dynamic_slice_in_dim(query_all, slot_index * FILE_BLOCK_SIZE, FILE_BLOCK_SIZE, 0)
            gradient_rows = lax.dynamic_slice_in_dim(incoming_gradient, slot_index * FILE_BLOCK_SIZE, FILE_BLOCK_SIZE, 0)
            reachable = lax.dynamic_index_in_dim(slot_mask, slot_index, 0, keepdims=False)
            live_keys = (reachable > 0.5).astype(jnp.int32)
            sort_order = jnp.argsort(1 - live_keys, stable=True)[:IMP + 1].astype(jnp.int32)
            key_live = jnp.take(live_keys, sort_order) > 0
            q_grad, key_value_block = block_grads(query_row_tensor, gradient_rows, key_block_list[sort_order], value_block_list[sort_order], sort_order, key_live, slot_index, softmax_scale)
            partial_sum = partial_sum.at[sort_order].add(key_value_block.reshape(IMP + 1, FILE_BLOCK_SIZE, column_counts))
            q_parts.append(q_grad)
        rounded = lowered(partial_sum).reshape(MICRO_LENGTH, column_counts)
        return (carried + rounded, jnp.concatenate(q_parts, axis=0))
    totals, q_grads = lax.scan(device_turn, jnp.zeros((MICRO_LENGTH, column_counts), jnp.float32), jnp.arange(N_CTX, dtype=jnp.int32))
    return (q_grads.reshape(MICRO_LENGTH, QUERY_HEADS * HEAD_DIMENSION), totals)

def reference(queries, keys, values, grad_a, grad_b, imports, block_ids):
    softmax_scale = 1.0 / math.sqrt(HEAD_DIMENSION)

    def section_fn(section_args):
        query_all, every_key, every_value, incoming_gradient, import_mask, block_order = section_args
        return section_micro(query_all, every_key, every_value, incoming_gradient, import_mask, block_order, softmax_scale)
    q_first, kv_first = lax.map(section_fn, (queries[0], keys[0], values[0], grad_a, imports[0], block_ids[0]))
    dq_a = q_first.astype(jnp.bfloat16)
    arrived = jnp.concatenate([dq_a[1:], jnp.zeros_like(dq_a[:1])], axis=0)
    upstream_b = (grad_b.astype(jnp.float32) + arrived.astype(jnp.float32)).astype(jnp.bfloat16)
    q_second, kv_second = lax.map(section_fn, (queries[1], keys[1], values[1], upstream_b, imports[1], block_ids[1]))
    kv_grads = jnp.stack([kv_first, kv_second]).astype(jnp.bfloat16)
    return (dq_a, q_second.astype(jnp.bfloat16), kv_grads)
```

```python
import math

import jax
import jax.numpy as jnp
from jax import lax
from jax.experimental import pallas as pl
from jax.experimental.pallas import tpu as pltpu
from jax.sharding import PartitionSpec as P

QUERY_HEADS = 20
KEY_VALUE_HEADS = 4
HEAD_DIMENSION = 128
FILE_BLOCK_SIZE = 128
MICRO_BATCHES = 2

GROUP = QUERY_HEADS // KEY_VALUE_HEADS
SIDES = 2
HALF_KV = KEY_VALUE_HEADS // SIDES
HALF_Q_WIDTH = HALF_KV * GROUP * HEAD_DIMENSION
HALF_KV_WIDTH = HALF_KV * HEAD_DIMENSION
STACK = GROUP * FILE_BLOCK_SIZE
negative_large = -1e30
SCALE = 1.0 / math.sqrt(HEAD_DIMENSION)
EXP2_SCALE = SCALE * math.log2(math.e)

NT = (((1,), (1,)), ((), ()))
NN = (((1,), (0,)), ((), ()))
TN = (((0,), (0,)), ((), ()))


def folded_order(lines):
    return [0] + list(range(1, lines, 2)) + list(range(2, lines, 2))[::-1]


def line_position(line, lines):
    odd = lax.rem(line, 2) == 1
    return jnp.where(line == 0, 0, jnp.where(odd, (line + 1) // 2, lines - line // 2))


def position_line(position, lines):
    return jnp.where(
        position == 0, 0, jnp.where(position <= lines // 2, 2 * position - 1, 2 * (lines - position))
    )


def fold_rows(tile, op):
    rows, columns = tile.shape
    return op(tile.reshape(rows // 8, 8, columns), axis=0)


def backward_kernel(lines, micro, with_arrived, *refs):
    side_count = SIDES
    tiles = lines * side_count
    refs = list(refs)
    imports_ref, ids_ref = refs[:2]
    q_refs, g_refs = refs[2:4], refs[4:6]
    at = 6
    arrived_refs = None
    if with_arrived:
        arrived_refs = refs[at : at + 2]
        at += 2
    kv_refs = refs[at : at + tiles]
    at += tiles
    dq_refs = refs[at : at + 2]
    at += 2
    dkv_refs = refs[at : at + tiles]
    at += tiles
    kv_all, q_stack, g_stack, scores, dprobs, dkv_sum, listing = refs[at:]

    me = lax.axis_index("ctx")
    line, side = me // side_count, lax.rem(me, side_count)
    position = line_position(line, lines)

    for tile in range(tiles):
        kv_all[tile] = kv_refs[tile][...]
    dkv_sum[...] = jnp.zeros_like(dkv_sum)

    for block in range(side_count):
        query_slot = line * side_count + (side if block == 0 else 1 - side)
        query_id = ids_ref[micro, 0, query_slot]
        count = jnp.int32(0)
        for step in range(lines):
            source = lax.rem(position - step + lines, lines)
            key_line = position_line(source, lines)
            for chain in range(side_count):
                if step == 0 and chain == block:
                    continue
                key_slot = key_line * side_count + (side if chain == 0 else 1 - side)
                key_id = ids_ref[micro, 0, key_slot]
                listing[block, count] = step * side_count + chain
                count = count + jnp.where(imports_ref[micro, 0, query_id, key_id] > 0, 1, 0)
        listing[block, tiles] = count

    triangle = lax.broadcasted_iota(jnp.int32, (FILE_BLOCK_SIZE, FILE_BLOCK_SIZE), 0) <= (
        lax.broadcasted_iota(jnp.int32, (FILE_BLOCK_SIZE, FILE_BLOCK_SIZE), 1)
    )
    allowed = jnp.concatenate([triangle] * GROUP, axis=1)

    for block in range(side_count):
        count = listing[block, tiles]
        for head in range(HALF_KV):
            for member in range(GROUP):
                rows = slice(member * FILE_BLOCK_SIZE, (member + 1) * FILE_BLOCK_SIZE)
                start = (head * GROUP + member) * HEAD_DIMENSION
                columns = slice(start, start + HEAD_DIMENSION)
                q_stack[rows, :] = q_refs[block][:, columns]
                upstream = g_refs[block][:, columns]
                if with_arrived:
                    upstream = (
                        upstream.astype(jnp.float32)
                        + arrived_refs[block][:, columns].astype(jnp.float32)
                    ).astype(jnp.bfloat16)
                g_stack[rows, :] = upstream
            key_columns = slice(head * HEAD_DIMENSION, (head + 1) * HEAD_DIMENSION)
            value_columns = slice(
                HALF_KV_WIDTH + head * HEAD_DIMENSION, HALF_KV_WIDTH + (head + 1) * HEAD_DIMENSION
            )

            def products(tile):
                score = lax.dot_general(
                    kv_all[tile, :, key_columns],
                    q_stack[...],
                    NT,
                    preferred_element_type=jnp.float32,
                )
                dprobs[tile] = lax.dot_general(
                    kv_all[tile, :, value_columns],
                    g_stack[...],
                    NT,
                    preferred_element_type=jnp.float32,
                )
                return score

            own = block
            score = jnp.where(allowed, products(own), negative_large)
            scores[own] = score

            def first(turn, largest):
                tile = listing[block, turn]
                score = products(tile)
                scores[tile] = score
                return jnp.maximum(largest, fold_rows(score, jnp.max))

            largest = lax.fori_loop(0, count, first, fold_rows(score, jnp.max))
            row_max = jnp.max(largest, axis=0, keepdims=True)

            def weigh(tile):
                weight = jnp.exp2((scores[tile] - row_max) * EXP2_SCALE)
                scores[tile] = weight
                return fold_rows(weight, jnp.sum), fold_rows(weight * dprobs[tile], jnp.sum)

            def second(turn, sums):
                added = weigh(listing[block, turn])
                return (sums[0] + added[0], sums[1] + added[1])

            sums = lax.fori_loop(0, count, second, weigh(own))
            inverse = 1.0 / jnp.sum(sums[0], axis=0, keepdims=True)
            delta = jnp.sum(sums[1], axis=0, keepdims=True) * inverse

            def spread(tile):
                prob = scores[tile] * inverse
                score_grad = (prob * (dprobs[tile] - delta)).astype(jnp.bfloat16)
                dkv_sum[tile, :, key_columns] += lax.dot_general(
                    score_grad, q_stack[...], NN, preferred_element_type=jnp.float32
                )
                dkv_sum[tile, :, value_columns] += lax.dot_general(
                    prob.astype(jnp.bfloat16), g_stack[...], NN, preferred_element_type=jnp.float32
                )
                return lax.dot_general(
                    kv_all[tile, :, key_columns], score_grad, TN, preferred_element_type=jnp.float32
                )

            def third(turn, total):
                return total + spread(listing[block, turn])

            dq_turned = lax.fori_loop(0, count, third, spread(own)) * SCALE
            for member in range(GROUP):
                start = (head * GROUP + member) * HEAD_DIMENSION
                part = dq_turned[:, member * FILE_BLOCK_SIZE : (member + 1) * FILE_BLOCK_SIZE]
                dq_refs[block][:, start : start + HEAD_DIMENSION] = part.T.astype(jnp.bfloat16)

    for tile in range(tiles):
        dkv_refs[tile][:, :HALF_KV_WIDTH] = (dkv_sum[tile, :, :HALF_KV_WIDTH] * SCALE).astype(
            jnp.bfloat16
        )
        dkv_refs[tile][:, HALF_KV_WIDTH:] = dkv_sum[tile, :, HALF_KV_WIDTH:].astype(jnp.bfloat16)


def backward(lines, micro, imports, block_ids, q_pair, g_pair, arrived_pair, kv_tiles):
    tiles = lines * SIDES
    with_arrived = arrived_pair is not None
    vmem = pl.BlockSpec(memory_space=pltpu.VMEM)
    smem = pl.BlockSpec(memory_space=pltpu.SMEM)
    operands = [imports, block_ids, *q_pair, *g_pair]
    if with_arrived:
        operands += arrived_pair
    operands += kv_tiles
    query_shape = jax.ShapeDtypeStruct((FILE_BLOCK_SIZE, HALF_Q_WIDTH), jnp.bfloat16)
    key_shape = jax.ShapeDtypeStruct((FILE_BLOCK_SIZE, 2 * HALF_KV_WIDTH), jnp.bfloat16)

    def body(*refs):
        backward_kernel(lines, micro, with_arrived, *refs)

    results = pl.pallas_call(
        body,
        out_shape=[query_shape] * 2 + [key_shape] * tiles,
        in_specs=[smem, smem] + [vmem] * (len(operands) - 2),
        out_specs=[vmem] * (2 + tiles),
        scratch_shapes=[
            pltpu.VMEM((tiles, FILE_BLOCK_SIZE, 2 * HALF_KV_WIDTH), jnp.bfloat16),
            pltpu.VMEM((STACK, HEAD_DIMENSION), jnp.bfloat16),
            pltpu.VMEM((STACK, HEAD_DIMENSION), jnp.bfloat16),
            pltpu.VMEM((tiles, FILE_BLOCK_SIZE, STACK), jnp.float32),
            pltpu.VMEM((tiles, FILE_BLOCK_SIZE, STACK), jnp.float32),
            pltpu.VMEM((tiles, FILE_BLOCK_SIZE, 2 * HALF_KV_WIDTH), jnp.float32),
            pltpu.SMEM((SIDES, tiles + 1), jnp.int32),
        ],
        compiler_params=pltpu.CompilerParams(vmem_limit_bytes=48 * 1024 * 1024),
        cost_estimate=pl.CostEstimate(flops=4 * 10**9, bytes_accessed=4 * 10**6, transcendentals=0),
    )(*operands)
    return results[:2], results[2:]


def on_device(queries, keys, values, grad_a, grad_b, imports, block_ids):
    devices = lax.axis_size("ctx")
    lines = devices // SIDES
    side = lax.rem(lax.axis_index("ctx"), SIDES)
    order = folded_order(lines)
    ring = [
        (order[i] * SIDES + s, order[(i + 1) % lines] * SIDES + s)
        for i in range(lines)
        for s in range(SIDES)
    ]
    pairs = [(i, i ^ 1) for i in range(devices)]
    pipe = lax.axis_size("pipe")
    back = [(i + 1, i) for i in range(pipe - 1)]

    def swap(block):
        return lax.ppermute(block, "ctx", pairs)

    def turn(block):
        return lax.ppermute(block, "ctx", ring)

    def split(rows, width):
        kept = lax.dynamic_slice_in_dim(rows, side * width, width, 1)
        given = lax.dynamic_slice_in_dim(rows, (1 - side) * width, width, 1)
        return kept, given

    def joined(kept, received):
        ordered = jnp.concatenate([kept, received], axis=1)
        crossed = jnp.concatenate([received, kept], axis=1)
        return jnp.where(side == 0, ordered, crossed)

    def gathered(micro):
        key_kept, key_given = split(keys[micro, 0], HALF_KV_WIDTH)
        value_kept, value_given = split(values[micro, 0], HALF_KV_WIDTH)
        own = jnp.concatenate([key_kept, value_kept], axis=1)
        other = swap(jnp.concatenate([key_given, value_given], axis=1))
        tiles = [own, other]
        for _ in range(1, lines):
            own, other = turn(own), turn(other)
            tiles += [own, other]
        return tiles

    def exchanged(rows):
        kept, given = split(rows, HALF_Q_WIDTH)
        return [kept, swap(given)]

    def scattered(parts):
        sums = []
        for chain in range(SIDES):
            total = parts[SIDES + chain] if lines > 1 else parts[chain]
            for step in list(range(2, lines)) + ([0] if lines > 1 else []):
                total = (
                    turn(total).astype(jnp.float32)
                    + parts[step * SIDES + chain].astype(jnp.float32)
                ).astype(jnp.bfloat16)
            sums.append(total)
        received = swap(sums[1])
        key_part = joined(sums[0][:, :HALF_KV_WIDTH], received[:, :HALF_KV_WIDTH])
        value_part = joined(sums[0][:, HALF_KV_WIDTH:], received[:, HALF_KV_WIDTH:])
        return jnp.concatenate([key_part, value_part], axis=1)

    tiles_a = gathered(0)
    q_a = exchanged(queries[0, 0])
    g_a = exchanged(grad_a[0])
    tiles_b = gathered(1)
    q_b = exchanged(queries[1, 0])
    g_b = exchanged(grad_b[0])

    dq_a, dkv_a = backward(lines, 0, imports, block_ids, q_a, g_a, None, tiles_a)
    arrived = [lax.ppermute(part, "pipe", back) for part in dq_a]
    dq_b, dkv_b = backward(lines, 1, imports, block_ids, q_b, g_b, arrived, tiles_b)
    out_a = joined(dq_a[0], swap(dq_a[1]))
    out_b = joined(dq_b[0], swap(dq_b[1]))
    kv = jnp.stack([scattered(dkv_a), scattered(dkv_b)])
    return (out_a[None], out_b[None], kv[:, None])


def solution(mesh):
    return jax.shard_map(
        on_device,
        mesh=mesh,
        in_specs=(
            P(None, "pipe", "ctx", None),
            P(None, "pipe", "ctx", None),
            P(None, "pipe", "ctx", None),
            P("pipe", "ctx", None),
            P("pipe", "ctx", None),
            P(None, "pipe", None, None),
            P(None, "pipe", None),
        ),
        out_specs=(P("pipe", "ctx", None), P("pipe", "ctx", None), P(None, "pipe", "ctx", None)),
        check_vma=False,
    )
```

```python
import math

import jax
import jax.numpy as jnp
from jax import lax
from jax.experimental import pallas as pl
from jax.experimental.pallas import tpu as pltpu
from jax.sharding import PartitionSpec as P

QUERY_HEADS = 20
KEY_VALUE_HEADS = 4
HEAD_DIMENSION = 128
FILE_BLOCK_SIZE = 128
MICRO_BATCHES = 2

GROUP = QUERY_HEADS // KEY_VALUE_HEADS
SIDES = 2
HALF_KV = KEY_VALUE_HEADS // SIDES
HALF_Q_WIDTH = HALF_KV * GROUP * HEAD_DIMENSION
HALF_KV_WIDTH = HALF_KV * HEAD_DIMENSION
STACK = GROUP * FILE_BLOCK_SIZE
negative_large = -1e30
SCALE = 1.0 / math.sqrt(HEAD_DIMENSION)
EXP2_SCALE = SCALE * math.log2(math.e)

NT = (((1,), (1,)), ((), ()))
NN = (((1,), (0,)), ((), ()))
TN = (((0,), (0,)), ((), ()))


def folded_order(lines):
    return [0] + list(range(1, lines, 2)) + list(range(2, lines, 2))[::-1]


def line_position(line, lines):
    odd = lax.rem(line, 2) == 1
    return jnp.where(line == 0, 0, jnp.where(odd, (line + 1) // 2, lines - line // 2))


def position_line(position, lines):
    return jnp.where(
        position == 0, 0, jnp.where(position <= lines // 2, 2 * position - 1, 2 * (lines - position))
    )


def fold_rows(tile, op):
    rows, columns = tile.shape
    return op(tile.reshape(rows // 8, 8, columns), axis=0)


def backward_kernel(lines, micro, with_arrived, kv_count, *refs):
    tiles = lines * SIDES
    refs = list(refs)
    imports_ref, ids_ref, q_ref, g_ref, received_ref = refs[:5]
    at = 5
    arrived_ref = None
    if with_arrived:
        arrived_ref = refs[at]
        at += 1
    kv_refs = refs[at : at + kv_count]
    at += kv_count
    dq_ref = refs[at]
    at += 1
    dkv_refs = refs[at : at + lines]
    at += lines
    packed, q_stack, g_stack, scores, dprobs, dkv_sum, listing = refs[at:]

    me = lax.axis_index("ctx")
    line, side = me // SIDES, lax.rem(me, SIDES)
    position = line_position(line, lines)
    lane = side * HALF_Q_WIDTH

    def tile_value(tile):
        if kv_count == tiles:
            return kv_refs[tile][...]
        return kv_refs[tile // SIDES][tile % SIDES]

    evens, chunks = [], []
    for block in range(SIDES):
        query_slot = line * SIDES + (side if block == 0 else 1 - side)
        query_id = ids_ref[micro, 0, query_slot]
        others = []
        total = jnp.int32(1)
        for tile in range(tiles):
            if tile == block:
                continue
            step, chain = tile // SIDES, tile % SIDES
            key_line = position_line(lax.rem(position - step + lines, lines), lines)
            key_slot = key_line * SIDES + (side if chain == 0 else 1 - side)
            key_id = ids_ref[micro, 0, key_slot]
            live = imports_ref[micro, 0, query_id, key_id] > 0
            others.append((tile, live))
            total = total + jnp.where(live, 1, 0)
        even = lax.rem(total, 2) == 0
        evens.append(even)
        chunks.append((total + 1) // 2)
        listing[block, 0] = block
        listing[block, 1] = block
        packed[block, 0, :FILE_BLOCK_SIZE] = tile_value(block)
        packed[block, 0, FILE_BLOCK_SIZE:] = tile_value(block)
        place = jnp.where(even, 1, 2)
        for tile, live in others:

            def take(block=block, place=place, tile=tile):
                listing[block, place] = tile
                rows = pl.ds(
                    pl.multiple_of(lax.rem(place, 2) * FILE_BLOCK_SIZE, FILE_BLOCK_SIZE),
                    FILE_BLOCK_SIZE,
                )
                packed[block, place // 2, rows] = tile_value(tile)

            pl.when(live)(take)
            place = place + jnp.where(live, 1, 0)

    dkv_sum[...] = jnp.zeros_like(dkv_sum)

    triangle = lax.broadcasted_iota(jnp.int32, (FILE_BLOCK_SIZE, FILE_BLOCK_SIZE), 0) <= (
        lax.broadcasted_iota(jnp.int32, (FILE_BLOCK_SIZE, FILE_BLOCK_SIZE), 1)
    )
    allowed = jnp.concatenate([triangle] * GROUP, axis=1)
    head_columns = [
        slice(head * HEAD_DIMENSION, (head + 1) * HEAD_DIMENSION) for head in range(HALF_KV)
    ]
    value_columns = [
        slice(HALF_KV_WIDTH + head * HEAD_DIMENSION, HALF_KV_WIDTH + (head + 1) * HEAD_DIMENSION)
        for head in range(HALF_KV)
    ]

    for block in range(SIDES):
        for head in range(HALF_KV):
            for member in range(GROUP):
                rows = slice(member * FILE_BLOCK_SIZE, (member + 1) * FILE_BLOCK_SIZE)
                start = (head * GROUP + member) * HEAD_DIMENSION
                columns = slice(start, start + HEAD_DIMENSION)
                if block == 0:
                    wide = pl.ds(pl.multiple_of(lane + start, HEAD_DIMENSION), HEAD_DIMENSION)
                    q_stack[head, rows, :] = q_ref[micro, 0, :, wide]
                    upstream = g_ref[0, :, wide]
                else:
                    q_stack[head, rows, :] = received_ref[0, :, columns]
                    upstream = received_ref[1, :, columns]
                if with_arrived:
                    upstream = (
                        upstream.astype(jnp.float32)
                        + arrived_ref[block, :, columns].astype(jnp.float32)
                    ).astype(jnp.bfloat16)
                g_stack[head, rows, :] = upstream

        def products(chunk, head):
            score = lax.dot_general(
                packed[block, chunk, :, head_columns[head]],
                q_stack[head],
                NT,
                preferred_element_type=jnp.float32,
            )
            dprobs[head, chunk] = lax.dot_general(
                packed[block, chunk, :, value_columns[head]],
                g_stack[head],
                NT,
                preferred_element_type=jnp.float32,
            )
            return score

        def first(chunk, largest):
            found = []
            for head in range(HALF_KV):
                score = products(chunk, head)
                scores[head, chunk] = score
                found.append(jnp.maximum(largest[head], fold_rows(score, jnp.max)))
            return tuple(found)

        largest = []
        for head in range(HALF_KV):
            score = products(0, head)
            score = jnp.concatenate(
                [
                    jnp.where(allowed, score[:FILE_BLOCK_SIZE], negative_large),
                    score[FILE_BLOCK_SIZE:] + jnp.where(evens[block], 0.0, negative_large),
                ],
                axis=0,
            )
            scores[head, 0] = score
            largest.append(fold_rows(score, jnp.max))
        largest = lax.fori_loop(1, chunks[block], first, tuple(largest))
        row_max = [jnp.max(value, axis=0, keepdims=True) for value in largest]

        def second(chunk, sums):
            found = []
            for head in range(HALF_KV):
                weight = jnp.exp2((scores[head, chunk] - row_max[head]) * EXP2_SCALE)
                scores[head, chunk] = weight
                found.append(sums[2 * head] + fold_rows(weight, jnp.sum))
                found.append(sums[2 * head + 1] + fold_rows(weight * dprobs[head, chunk], jnp.sum))
            return tuple(found)

        nothing = jnp.zeros((8, STACK), jnp.float32)
        sums = lax.fori_loop(0, chunks[block], second, (nothing,) * (2 * HALF_KV))
        inverse = [1.0 / jnp.sum(sums[2 * h], axis=0, keepdims=True) for h in range(HALF_KV)]
        delta = [
            jnp.sum(sums[2 * h + 1], axis=0, keepdims=True) * inverse[h] for h in range(HALF_KV)
        ]

        def third(chunk, totals):
            found = []
            tile_pair = [listing[block, 2 * chunk], listing[block, 2 * chunk + 1]]
            for head in range(HALF_KV):
                prob = scores[head, chunk] * inverse[head]
                score_grad = (prob * (dprobs[head, chunk] - delta[head])).astype(jnp.bfloat16)
                key_part = lax.dot_general(
                    score_grad, q_stack[head], NN, preferred_element_type=jnp.float32
                )
                value_part = lax.dot_general(
                    prob.astype(jnp.bfloat16), g_stack[head], NN, preferred_element_type=jnp.float32
                )
                for place in range(2):
                    rows = slice(place * FILE_BLOCK_SIZE, (place + 1) * FILE_BLOCK_SIZE)
                    dkv_sum[tile_pair[place], :, head_columns[head]] += key_part[rows]
                    dkv_sum[tile_pair[place], :, value_columns[head]] += value_part[rows]
                found.append(
                    totals[head]
                    + lax.dot_general(
                        packed[block, chunk, :, head_columns[head]],
                        score_grad,
                        TN,
                        preferred_element_type=jnp.float32,
                    )
                )
            return tuple(found)

        empty = jnp.zeros((HEAD_DIMENSION, STACK), jnp.float32)
        dq_turned = lax.fori_loop(0, chunks[block], third, (empty,) * HALF_KV)
        for head in range(HALF_KV):
            for member in range(GROUP):
                start = (head * GROUP + member) * HEAD_DIMENSION
                part = dq_turned[head][:, member * FILE_BLOCK_SIZE : (member + 1) * FILE_BLOCK_SIZE]
                dq_ref[block, :, start : start + HEAD_DIMENSION] = (part.T * SCALE).astype(
                    jnp.bfloat16
                )

    for tile in range(tiles):
        out, chain = dkv_refs[tile // SIDES], tile % SIDES
        out[chain, :, :HALF_KV_WIDTH] = (dkv_sum[tile, :, :HALF_KV_WIDTH] * SCALE).astype(
            jnp.bfloat16
        )
        out[chain, :, HALF_KV_WIDTH:] = dkv_sum[tile, :, HALF_KV_WIDTH:].astype(jnp.bfloat16)


def backward(lines, micro, imports, block_ids, queries, gradient, received, arrived, kv_parts):
    tiles = lines * SIDES
    with_arrived = arrived is not None
    vmem = pl.BlockSpec(memory_space=pltpu.VMEM)
    smem = pl.BlockSpec(memory_space=pltpu.SMEM)
    operands = [imports, block_ids, queries, gradient, received]
    if with_arrived:
        operands.append(arrived)
    operands += kv_parts
    query_shape = (SIDES, FILE_BLOCK_SIZE, HALF_Q_WIDTH)
    key_shape = (SIDES, FILE_BLOCK_SIZE, 2 * HALF_KV_WIDTH)

    def body(*refs):
        backward_kernel(lines, micro, with_arrived, len(kv_parts), *refs)

    stacked = (HALF_KV, STACK, HEAD_DIMENSION)
    squares = (HALF_KV, tiles // 2, 2 * FILE_BLOCK_SIZE, STACK)
    results = pl.pallas_call(
        body,
        out_shape=[jax.ShapeDtypeStruct(query_shape, jnp.bfloat16)]
        + [jax.ShapeDtypeStruct(key_shape, jnp.bfloat16)] * lines,
        in_specs=[smem, smem] + [vmem] * (len(operands) - 2),
        out_specs=[vmem] * (1 + lines),
        scratch_shapes=[
            pltpu.VMEM((SIDES, tiles // 2, 2 * FILE_BLOCK_SIZE, 2 * HALF_KV_WIDTH), jnp.bfloat16),
            pltpu.VMEM(stacked, jnp.bfloat16),
            pltpu.VMEM(stacked, jnp.bfloat16),
            pltpu.VMEM(squares, jnp.float32),
            pltpu.VMEM(squares, jnp.float32),
            pltpu.VMEM((tiles, FILE_BLOCK_SIZE, 2 * HALF_KV_WIDTH), jnp.float32),
            pltpu.SMEM((SIDES, tiles), jnp.int32),
        ],
        compiler_params=pltpu.CompilerParams(vmem_limit_bytes=48 * 1024 * 1024),
        cost_estimate=pl.CostEstimate(
            flops=10 * 10**9, bytes_accessed=4 * 10**6, transcendentals=0
        ),
    )(*operands)
    return results[0], results[1:]


def on_device(queries, keys, values, grad_a, grad_b, imports, block_ids):
    devices = lax.axis_size("ctx")
    lines = devices // SIDES
    side = lax.rem(lax.axis_index("ctx"), SIDES)
    order = folded_order(lines)
    pairs = [(i, i ^ 1) for i in range(devices)]
    pipe = lax.axis_size("pipe")
    back = [(i + 1, i) for i in range(pipe - 1)]

    def swap(block):
        return lax.ppermute(block, "ctx", pairs)

    def turn(block, distance=1):
        route = [
            (order[i] * SIDES + s, order[(i + distance) % lines] * SIDES + s)
            for i in range(lines)
            for s in range(SIDES)
        ]
        return lax.ppermute(block, "ctx", route)

    def part(rows, width, of_side):
        return lax.dynamic_slice_in_dim(rows, of_side * width, width, 1)

    def key_part(micro, key_rows, value_rows, of_side):
        return jnp.concatenate(
            [
                part(key_rows[micro, 0], HALF_KV_WIDTH, of_side),
                part(value_rows[micro, 0], HALF_KV_WIDTH, of_side),
            ],
            axis=1,
        )

    def row_part(query_rows, gradient_rows):
        return jnp.stack(
            [
                part(query_rows, HALF_Q_WIDTH, 1 - side),
                part(gradient_rows, HALF_Q_WIDTH, 1 - side),
            ]
        )

    def joined(kept, received):
        ordered = jnp.concatenate([kept, received], axis=1)
        crossed = jnp.concatenate([received, kept], axis=1)
        return jnp.where(side == 0, ordered, crossed)

    def after(value, earlier):
        return lax.optimization_barrier((value, earlier))[0]

    def finished(sums):
        received = swap(sums[1])
        key_half = joined(sums[0][:, :HALF_KV_WIDTH], received[:, :HALF_KV_WIDTH])
        value_half = joined(sums[0][:, HALF_KV_WIDTH:], received[:, HALF_KV_WIDTH:])
        return jnp.concatenate([key_half, value_half], axis=1)

    def summed(parts, moved):
        total = parts[0].astype(jnp.float32)
        for block in moved:
            total = total + block.astype(jnp.float32)
        return total.astype(jnp.bfloat16)

    own = key_part(0, keys, values, side)
    given = key_part(0, keys, values, 1 - side)
    rows_a = swap(row_part(queries[0, 0], grad_a[0]))
    other = swap(given)
    tiles_a = [own, other]
    for _ in range(1, lines):
        own, other = turn(own), turn(other)
        tiles_a += [own, other]

    keys_b, values_b = lax.optimization_barrier((keys, values, tiles_a[1]))[:2]
    own_b = key_part(1, keys_b, values_b, side)
    other_b = swap(key_part(1, keys_b, values_b, 1 - side))
    unit_b = jnp.stack([own_b, other_b])
    unit_b = after(unit_b, tiles_a[2 * lines - 3]) if lines > 1 else unit_b
    queries_b, gradient_b = lax.optimization_barrier((queries, grad_b, tiles_a[3]))[:2]
    rows_b = swap(row_part(queries_b[1, 0], gradient_b[0]))
    units_b = [unit_b] + [turn(unit_b, step) for step in range(1, lines)]
    rows_a = after(rows_a, unit_b)

    dq_a, dkv_a = backward(
        lines, 0, imports, block_ids, queries, grad_a, rows_a, None, tiles_a
    )
    if lines > 1:
        dq_a, units_b[1] = lax.optimization_barrier((dq_a, units_b[1]))
    arrived = lax.ppermute(dq_a, "pipe", back)
    tied = lax.optimization_barrier((*units_b, *dkv_a))
    units_b, dkv_a = list(tied[:lines]), list(tied[lines:])
    back_a = swap(dq_a[1])
    moved_a = [turn(dkv_a[step], lines - step) for step in range(1, lines)]
    dq_b, dkv_b = backward(
        lines, 1, imports, block_ids, queries, grad_b, rows_b, arrived, units_b
    )
    moved_b = [turn(dkv_b[step], lines - step) for step in range(1, lines)]
    back_b = swap(dq_b[1])
    held = lax.optimization_barrier((moved_b[0], back_a, dkv_a[0], *moved_a))
    moved_b[0] = held[0]
    out_a = joined(dq_a[0], held[1])
    kv_a = finished(summed([held[2]], held[3:]))
    out_b = joined(dq_b[0], back_b)
    kv_b = finished(summed([dkv_b[0]], moved_b))
    kv = jnp.stack([kv_a, kv_b])
    return (out_a[None], out_b[None], kv[:, None])


def solution(mesh):
    return jax.shard_map(
        on_device,
        mesh=mesh,
        in_specs=(
            P(None, "pipe", "ctx", None),
            P(None, "pipe", "ctx", None),
            P(None, "pipe", "ctx", None),
            P("pipe", "ctx", None),
            P("pipe", "ctx", None),
            P(None, "pipe", None, None),
            P(None, "pipe", None),
        ),
        out_specs=(P("pipe", "ctx", None), P("pipe", "ctx", None), P(None, "pipe", "ctx", None)),
        check_vma=False,
    )
```

```python
import math

import jax
import jax.numpy as jnp
from jax import lax
from jax.experimental import pallas as pl
from jax.experimental.pallas import tpu as pltpu
from jax.sharding import PartitionSpec as P

QUERY_HEADS = 20
KEY_VALUE_HEADS = 4
HEAD_DIMENSION = 128
FILE_BLOCK_SIZE = 128
MICRO_BATCHES = 2

GROUP = QUERY_HEADS // KEY_VALUE_HEADS
SIDES = 2
HALF_KV = KEY_VALUE_HEADS // SIDES
HALF_Q_WIDTH = HALF_KV * GROUP * HEAD_DIMENSION
HALF_KV_WIDTH = HALF_KV * HEAD_DIMENSION
STACK = GROUP * FILE_BLOCK_SIZE
negative_large = -1e30
SCALE = 1.0 / math.sqrt(HEAD_DIMENSION)
EXP2_SCALE = SCALE * math.log2(math.e)

NT = (((1,), (1,)), ((), ()))
NN = (((1,), (0,)), ((), ()))
TN = (((0,), (0,)), ((), ()))


def line_masks(lines):
    masks = []
    while lines > 1:
        masks.append(lines - 1)
        lines //= 2
    return masks


def line_offsets(lines):
    offsets = [0]
    for mask in line_masks(lines):
        offsets += [offset ^ mask for offset in offsets]
    return offsets


def fold_rows(tile, op):
    rows, columns = tile.shape
    return op(tile.reshape(rows // 8, 8, columns), axis=0)


def backward_kernel(lines, micro, with_arrived, kv_count, *refs):
    tiles = lines * SIDES
    refs = list(refs)
    imports_ref, ids_ref, q_ref, g_ref, received_ref = refs[:5]
    at = 5
    arrived_ref = None
    if with_arrived:
        arrived_ref = refs[at]
        at += 1
    kv_refs = refs[at : at + kv_count]
    at += kv_count
    dq_ref = refs[at]
    at += 1
    dkv_refs = refs[at : at + lines]
    at += lines
    packed, q_stack, g_stack, scores, dprobs, dkv_sum, listing = refs[at:]

    me = lax.axis_index("ctx")
    line, side = me // SIDES, lax.rem(me, SIDES)
    offsets = line_offsets(lines)
    lane = side * HALF_Q_WIDTH

    def tile_value(tile):
        if kv_count == tiles:
            return kv_refs[tile][...]
        return kv_refs[tile // SIDES][tile % SIDES]

    evens, chunks = [], []
    for block in range(SIDES):
        query_slot = line * SIDES + (side if block == 0 else 1 - side)
        query_id = ids_ref[micro, 0, query_slot]
        others = []
        total = jnp.int32(1)
        for tile in range(tiles):
            if tile == block:
                continue
            step, chain = tile // SIDES, tile % SIDES
            key_line = jnp.bitwise_xor(line, offsets[step])
            key_slot = key_line * SIDES + (side if chain == 0 else 1 - side)
            key_id = ids_ref[micro, 0, key_slot]
            live = imports_ref[micro, 0, query_id, key_id] > 0
            others.append((tile, live))
            total = total + jnp.where(live, 1, 0)
        even = lax.rem(total, 2) == 0
        evens.append(even)
        chunks.append((total + 1) // 2)
        listing[block, 0] = block
        listing[block, 1] = block
        packed[block, 0, :FILE_BLOCK_SIZE] = tile_value(block)
        packed[block, 0, FILE_BLOCK_SIZE:] = tile_value(block)
        place = jnp.where(even, 1, 2)
        for tile, live in others:

            def take(block=block, place=place, tile=tile):
                listing[block, place] = tile
                rows = pl.ds(
                    pl.multiple_of(lax.rem(place, 2) * FILE_BLOCK_SIZE, FILE_BLOCK_SIZE),
                    FILE_BLOCK_SIZE,
                )
                packed[block, place // 2, rows] = tile_value(tile)

            pl.when(live)(take)
            place = place + jnp.where(live, 1, 0)

    dkv_sum[...] = jnp.zeros_like(dkv_sum)

    triangle = lax.broadcasted_iota(jnp.int32, (FILE_BLOCK_SIZE, FILE_BLOCK_SIZE), 0) <= (
        lax.broadcasted_iota(jnp.int32, (FILE_BLOCK_SIZE, FILE_BLOCK_SIZE), 1)
    )
    allowed = jnp.concatenate([triangle] * GROUP, axis=1)
    head_columns = [
        slice(head * HEAD_DIMENSION, (head + 1) * HEAD_DIMENSION) for head in range(HALF_KV)
    ]
    value_columns = [
        slice(HALF_KV_WIDTH + head * HEAD_DIMENSION, HALF_KV_WIDTH + (head + 1) * HEAD_DIMENSION)
        for head in range(HALF_KV)
    ]

    for block in range(SIDES):
        for head in range(HALF_KV):
            for member in range(GROUP):
                rows = slice(member * FILE_BLOCK_SIZE, (member + 1) * FILE_BLOCK_SIZE)
                start = (head * GROUP + member) * HEAD_DIMENSION
                columns = slice(start, start + HEAD_DIMENSION)
                if block == 0:
                    wide = pl.ds(pl.multiple_of(lane + start, HEAD_DIMENSION), HEAD_DIMENSION)
                    q_stack[head, rows, :] = q_ref[micro, 0, :, wide]
                    upstream = g_ref[0, :, wide]
                else:
                    q_stack[head, rows, :] = received_ref[0, :, columns]
                    upstream = received_ref[1, :, columns]
                if with_arrived:
                    upstream = (
                        upstream.astype(jnp.float32)
                        + arrived_ref[block, :, columns].astype(jnp.float32)
                    ).astype(jnp.bfloat16)
                g_stack[head, rows, :] = upstream

        def products(chunk, head):
            score = lax.dot_general(
                packed[block, chunk, :, head_columns[head]],
                q_stack[head],
                NT,
                preferred_element_type=jnp.float32,
            )
            dprobs[head, chunk] = lax.dot_general(
                packed[block, chunk, :, value_columns[head]],
                g_stack[head],
                NT,
                preferred_element_type=jnp.float32,
            )
            return score

        def first(chunk, largest):
            found = []
            for head in range(HALF_KV):
                score = products(chunk, head)
                scores[head, chunk] = score
                found.append(jnp.maximum(largest[head], fold_rows(score, jnp.max)))
            return tuple(found)

        largest = []
        for head in range(HALF_KV):
            score = products(0, head)
            score = jnp.concatenate(
                [
                    jnp.where(allowed, score[:FILE_BLOCK_SIZE], negative_large),
                    score[FILE_BLOCK_SIZE:] + jnp.where(evens[block], 0.0, negative_large),
                ],
                axis=0,
            )
            scores[head, 0] = score
            largest.append(fold_rows(score, jnp.max))
        largest = lax.fori_loop(1, chunks[block], first, tuple(largest))
        row_max = [jnp.max(value, axis=0, keepdims=True) for value in largest]

        def second(chunk, sums):
            found = []
            for head in range(HALF_KV):
                weight = jnp.exp2((scores[head, chunk] - row_max[head]) * EXP2_SCALE)
                scores[head, chunk] = weight
                found.append(sums[2 * head] + fold_rows(weight, jnp.sum))
                found.append(sums[2 * head + 1] + fold_rows(weight * dprobs[head, chunk], jnp.sum))
            return tuple(found)

        nothing = jnp.zeros((8, STACK), jnp.float32)
        sums = lax.fori_loop(0, chunks[block], second, (nothing,) * (2 * HALF_KV))
        inverse = [1.0 / jnp.sum(sums[2 * h], axis=0, keepdims=True) for h in range(HALF_KV)]
        delta = [
            jnp.sum(sums[2 * h + 1], axis=0, keepdims=True) * inverse[h] for h in range(HALF_KV)
        ]

        def third(chunk, totals):
            found = []
            tile_pair = [listing[block, 2 * chunk], listing[block, 2 * chunk + 1]]
            for head in range(HALF_KV):
                prob = scores[head, chunk] * inverse[head]
                score_grad = (prob * (dprobs[head, chunk] - delta[head])).astype(jnp.bfloat16)
                key_part = lax.dot_general(
                    score_grad, q_stack[head], NN, preferred_element_type=jnp.float32
                )
                value_part = lax.dot_general(
                    prob.astype(jnp.bfloat16), g_stack[head], NN, preferred_element_type=jnp.float32
                )
                for place in range(2):
                    rows = slice(place * FILE_BLOCK_SIZE, (place + 1) * FILE_BLOCK_SIZE)
                    dkv_sum[tile_pair[place], :, head_columns[head]] += key_part[rows]
                    dkv_sum[tile_pair[place], :, value_columns[head]] += value_part[rows]
                found.append(
                    totals[head]
                    + lax.dot_general(
                        packed[block, chunk, :, head_columns[head]],
                        score_grad,
                        TN,
                        preferred_element_type=jnp.float32,
                    )
                )
            return tuple(found)

        empty = jnp.zeros((HEAD_DIMENSION, STACK), jnp.float32)
        dq_turned = lax.fori_loop(0, chunks[block], third, (empty,) * HALF_KV)
        for head in range(HALF_KV):
            for member in range(GROUP):
                start = (head * GROUP + member) * HEAD_DIMENSION
                part = dq_turned[head][:, member * FILE_BLOCK_SIZE : (member + 1) * FILE_BLOCK_SIZE]
                dq_ref[block, :, start : start + HEAD_DIMENSION] = (part.T * SCALE).astype(
                    jnp.bfloat16
                )

    for tile in range(tiles):
        out, chain = dkv_refs[tile // SIDES], tile % SIDES
        out[chain, :, :HALF_KV_WIDTH] = (dkv_sum[tile, :, :HALF_KV_WIDTH] * SCALE).astype(
            jnp.bfloat16
        )
        out[chain, :, HALF_KV_WIDTH:] = dkv_sum[tile, :, HALF_KV_WIDTH:].astype(jnp.bfloat16)


def backward(lines, micro, imports, block_ids, queries, gradient, received, arrived, kv_parts):
    tiles = lines * SIDES
    with_arrived = arrived is not None
    vmem = pl.BlockSpec(memory_space=pltpu.VMEM)
    smem = pl.BlockSpec(memory_space=pltpu.SMEM)
    operands = [imports, block_ids, queries, gradient, received]
    if with_arrived:
        operands.append(arrived)
    operands += kv_parts
    query_shape = (SIDES, FILE_BLOCK_SIZE, HALF_Q_WIDTH)
    key_shape = (SIDES, FILE_BLOCK_SIZE, 2 * HALF_KV_WIDTH)

    def body(*refs):
        backward_kernel(lines, micro, with_arrived, len(kv_parts), *refs)

    stacked = (HALF_KV, STACK, HEAD_DIMENSION)
    squares = (HALF_KV, tiles // 2, 2 * FILE_BLOCK_SIZE, STACK)
    scratch = [
        pltpu.VMEM((SIDES, tiles // 2, 2 * FILE_BLOCK_SIZE, 2 * HALF_KV_WIDTH), jnp.bfloat16),
        pltpu.VMEM(stacked, jnp.bfloat16),
        pltpu.VMEM(stacked, jnp.bfloat16),
        pltpu.VMEM(squares, jnp.float32),
        pltpu.VMEM(squares, jnp.float32),
        pltpu.VMEM((tiles, FILE_BLOCK_SIZE, 2 * HALF_KV_WIDTH), jnp.float32),
    ]
    needed = sum(math.prod(block.shape) * block.dtype.itemsize for block in scratch)
    needed += sum(math.prod(block.shape) * 2 for block in operands[2:])
    needed += math.prod(query_shape) * 2 + lines * math.prod(key_shape) * 2
    results = pl.pallas_call(
        body,
        out_shape=[jax.ShapeDtypeStruct(query_shape, jnp.bfloat16)]
        + [jax.ShapeDtypeStruct(key_shape, jnp.bfloat16)] * lines,
        in_specs=[smem, smem] + [vmem] * (len(operands) - 2),
        out_specs=[vmem] * (1 + lines),
        scratch_shapes=scratch + [pltpu.SMEM((SIDES, tiles), jnp.int32)],
        compiler_params=pltpu.CompilerParams(vmem_limit_bytes=needed + 6 * 1024 * 1024),
        cost_estimate=pl.CostEstimate(
            flops=10 * 10**9, bytes_accessed=4 * 10**6, transcendentals=0
        ),
    )(*operands)
    return results[0], results[1:]


def side_columns(of_side, width, start=0):
    return pl.ds(pl.multiple_of(start + of_side * width, HEAD_DIMENSION), width)


def my_side():
    return lax.rem(lax.axis_index("ctx"), SIDES)


def small_call(kernel, shapes, operands):
    vmem = pl.BlockSpec(memory_space=pltpu.VMEM)
    moved = sum(math.prod(block.shape) * 2 for block in operands)
    return pl.pallas_call(
        kernel,
        out_shape=[jax.ShapeDtypeStruct(shape, jnp.bfloat16) for shape in shapes],
        in_specs=[vmem] * len(operands),
        out_specs=[vmem] * len(shapes),
        compiler_params=pltpu.CompilerParams(vmem_limit_bytes=2 * moved + 4 * 1024 * 1024),
        cost_estimate=pl.CostEstimate(flops=0, bytes_accessed=2 * moved, transcendentals=0),
    )(*operands)


def split_keys_kernel(key_ref, value_ref, own_a_ref, own_b_ref, given_ref):
    side = my_side()
    own_refs = (own_a_ref, own_b_ref)
    for micro in range(MICRO_BATCHES):
        for place, ref in enumerate((key_ref, value_ref)):
            columns = slice(place * HALF_KV_WIDTH, (place + 1) * HALF_KV_WIDTH)
            own_refs[micro][:, columns] = ref[micro, 0, :, side_columns(side, HALF_KV_WIDTH)]
            given_ref[micro, :, columns] = ref[micro, 0, :, side_columns(1 - side, HALF_KV_WIDTH)]


def split_rows_kernel(micro, query_ref, gradient_ref, given_ref):
    columns = side_columns(1 - my_side(), HALF_Q_WIDTH)
    given_ref[0] = query_ref[micro, 0, :, columns]
    given_ref[1] = gradient_ref[0, :, columns]


def join_rows_kernel(own_ref, received_ref, out_ref):
    side = my_side()
    out_ref[0, :, side_columns(side, HALF_Q_WIDTH)] = own_ref[0]
    out_ref[0, :, side_columns(1 - side, HALF_Q_WIDTH)] = received_ref[...]


def assemble_kernel(sum_ref, crossed_ref, local_ref, *refs):
    *moved_refs, out_ref = refs
    half = len(moved_refs) // 2
    side = my_side()
    for micro in range(MICRO_BATCHES):
        if micro == 0:
            halves = (sum_ref[0], crossed_ref[...])
        else:
            halves = []
            for parts in (
                [local_ref[0]] + [ref[...] for ref in moved_refs[:half]],
                [ref[...] for ref in moved_refs[half:]],
            ):
                total = parts[0].astype(jnp.float32)
                for block in parts[1:]:
                    total = total + block.astype(jnp.float32)
                halves.append(total.astype(jnp.bfloat16))
        for total, of_side in zip(halves, (side, 1 - side)):
            for kind in range(2):
                start = kind * KEY_VALUE_HEADS * HEAD_DIMENSION
                out_ref[micro, 0, :, side_columns(of_side, HALF_KV_WIDTH, start)] = total[
                    :, kind * HALF_KV_WIDTH : (kind + 1) * HALF_KV_WIDTH
                ]


def on_device(queries, keys, values, grad_a, grad_b, imports, block_ids):
    devices = lax.axis_size("ctx")
    lines = devices // SIDES
    masks = line_masks(lines)
    offsets = line_offsets(lines)
    pipe = lax.axis_size("pipe")
    key_shape = (FILE_BLOCK_SIZE, 2 * HALF_KV_WIDTH)
    row_shape = (FILE_BLOCK_SIZE, HALF_Q_WIDTH)

    def moved(block, mask, crossing=0):
        route = [(i, i ^ (mask * SIDES + crossing)) for i in range(devices)]
        return lax.ppermute(block, "ctx", route)

    def swap(block):
        return moved(block, 0, 1)

    def down(block):
        return lax.ppermute(block, "pipe", [(i + 1, i) for i in range(pipe - 1)])

    def given_rows(micro, query_rows, gradient_rows):
        def kernel(*refs):
            split_rows_kernel(micro, *refs)

        return small_call(kernel, [(2,) + row_shape], [query_rows, gradient_rows])[0]

    def joined(own, received):
        shape = (1, FILE_BLOCK_SIZE, SIDES * HALF_Q_WIDTH)
        return small_call(join_rows_kernel, [shape], [own, received])[0]

    def together(*values):
        return list(lax.optimization_barrier(values))

    def add(*blocks):
        total = blocks[0].astype(jnp.float32)
        for block in blocks[1:]:
            total = total + block.astype(jnp.float32)
        return total.astype(jnp.bfloat16)

    def gathered(unit):
        units = [unit]
        for mask in masks:
            units += [moved(block, mask) for block in units]
        return units

    def nearer_sums(parts):
        held = {offset: [part] for offset, part in zip(offsets, parts)}
        for level in range(len(masks) - 1, 0, -1):
            kept = offsets[: 1 << level]
            held = {
                offset: [add(*held[offset]), moved(add(*held[offset ^ masks[level]]), masks[level])]
                for offset in reversed(kept)
            }
        return held

    own, own_b, given = small_call(
        split_keys_kernel, [key_shape, key_shape, (MICRO_BATCHES,) + key_shape], [keys, values]
    )
    others = swap(given)
    rows_a = swap(given_rows(0, queries, grad_a))
    tiles_a = []
    for pair in zip(gathered(own), gathered(others[0])):
        tiles_a += pair

    queries_b, gradient_b, _ = together(queries, grad_b, tiles_a[2])
    rows_b = swap(given_rows(1, queries_b, gradient_b))
    unit_b, rows_a, _ = together(jnp.stack([own_b, others[1]]), rows_a, tiles_a[2])
    early = [moved(unit_b, mask) for mask in masks]

    dq_a, dkv_a = backward(
        lines, 0, imports, block_ids, queries, grad_a, rows_a, None, tiles_a
    )
    dq_a, *early = together(dq_a, *early)
    arrived = down(dq_a)
    units_b = [unit_b]
    for mask, fresh in zip(masks, early):
        units_b += [fresh] + [moved(block, mask) for block in units_b[1:]]
    rest = together(*units_b, *dkv_a)
    units_b, dkv_a = rest[:lines], rest[lines:]
    moved_a = [moved(part, offset) for part, offset in zip(dkv_a[1:], offsets[1:])]
    back_a = swap(dq_a[1])
    dq_b, dkv_b = backward(
        lines, 1, imports, block_ids, queries, grad_b, rows_b, arrived, units_b
    )
    held_b = nearer_sums(dkv_b)
    near_b, back_a, own_a, *moved_a = together(held_b[masks[0]][-1], back_a, dkv_a[0], *moved_a)
    held_b[masks[0]][-1] = near_b
    far_b, local_b = add(*held_b[masks[0]]), add(*held_b[0])
    pieces_b = [
        local_b,
        moved(far_b[0], masks[0]),
        moved(far_b[1], masks[0], 1),
        swap(local_b[1]),
    ]
    sum_a = add(own_a, *moved_a)
    crossed_a = swap(sum_a[1])
    back_b = swap(dq_b[1])
    out_a = joined(dq_a, back_a)
    out_b = joined(dq_b, back_b)
    kv_shape = (MICRO_BATCHES, 1, FILE_BLOCK_SIZE, 2 * KEY_VALUE_HEADS * HEAD_DIMENSION)
    kv = small_call(assemble_kernel, [kv_shape], [sum_a, crossed_a, *pieces_b])[0]
    return out_a, out_b, kv


def solution(mesh):
    return jax.shard_map(
        on_device,
        mesh=mesh,
        in_specs=(
            P(None, "pipe", "ctx", None),
            P(None, "pipe", "ctx", None),
            P(None, "pipe", "ctx", None),
            P("pipe", "ctx", None),
            P("pipe", "ctx", None),
            P(None, "pipe", None, None),
            P(None, "pipe", None),
        ),
        out_specs=(P("pipe", "ctx", None), P("pipe", "ctx", None), P(None, "pipe", "ctx", None)),
        check_vma=False,
    )
```

```python
import math

import jax
import jax.numpy as jnp
from jax import lax
from jax.experimental import pallas as pl
from jax.experimental.pallas import tpu as pltpu
from jax.sharding import PartitionSpec as P

QUERY_HEADS = 20
KEY_VALUE_HEADS = 4
HEAD_DIMENSION = 128
FILE_BLOCK_SIZE = 128
MICRO_BATCHES = 2

GROUP = QUERY_HEADS // KEY_VALUE_HEADS
SIDES = 2
HALF_KV = KEY_VALUE_HEADS // SIDES
HALF_Q_WIDTH = HALF_KV * GROUP * HEAD_DIMENSION
HALF_KV_WIDTH = HALF_KV * HEAD_DIMENSION
STACK = GROUP * FILE_BLOCK_SIZE
negative_large = -1e30
SCALE = 1.0 / math.sqrt(HEAD_DIMENSION)
EXP2_SCALE = SCALE * math.log2(math.e)

NT = (((1,), (1,)), ((), ()))
NN = (((1,), (0,)), ((), ()))
TN = (((0,), (0,)), ((), ()))


def line_masks(lines):
    masks = []
    while lines > 1:
        masks.append(lines - 1)
        lines //= 2
    return masks


def line_offsets(lines):
    offsets = [0]
    for mask in line_masks(lines):
        offsets += [offset ^ mask for offset in offsets]
    return offsets


def fold_rows(tile, op):
    rows, columns = tile.shape
    return op(tile.reshape(rows // 8, 8, columns), axis=0)


def backward_kernel(lines, micro, with_arrived, kv_count, *refs):
    tiles = lines * SIDES
    refs = list(refs)
    imports_ref, ids_ref, q_ref, g_ref, received_ref = refs[:5]
    at = 5
    arrived_ref = None
    if with_arrived:
        arrived_ref = refs[at]
        at += 1
    kv_refs = refs[at : at + kv_count]
    at += kv_count
    dq_ref = refs[at]
    at += 1
    dkv_refs = refs[at : at + lines]
    at += lines
    packed, q_stack, g_stack, scores, dprobs, dkv_sum, listing = refs[at:]

    me = lax.axis_index("ctx")
    line, side = me // SIDES, lax.rem(me, SIDES)
    offsets = line_offsets(lines)
    lane = side * HALF_Q_WIDTH

    def tile_value(tile):
        if kv_count == tiles:
            return kv_refs[tile][...]
        return kv_refs[tile // SIDES][tile % SIDES]

    evens, chunks = [], []
    for block in range(SIDES):
        query_slot = line * SIDES + (side if block == 0 else 1 - side)
        query_id = ids_ref[micro, 0, query_slot]
        others = []
        total = jnp.int32(1)
        for tile in range(tiles):
            if tile == block:
                continue
            step, chain = tile // SIDES, tile % SIDES
            key_line = jnp.bitwise_xor(line, offsets[step])
            key_slot = key_line * SIDES + (side if chain == 0 else 1 - side)
            key_id = ids_ref[micro, 0, key_slot]
            live = imports_ref[micro, 0, query_id, key_id] > 0
            others.append((tile, live))
            total = total + jnp.where(live, 1, 0)
        even = lax.rem(total, 2) == 0
        evens.append(even)
        chunks.append((total + 1) // 2)
        listing[block, 0] = block
        listing[block, 1] = block
        packed[block, 0, :FILE_BLOCK_SIZE] = tile_value(block)
        packed[block, 0, FILE_BLOCK_SIZE:] = tile_value(block)
        place = jnp.where(even, 1, 2)
        for tile, live in others:

            def take(block=block, place=place, tile=tile):
                listing[block, place] = tile
                rows = pl.ds(
                    pl.multiple_of(lax.rem(place, 2) * FILE_BLOCK_SIZE, FILE_BLOCK_SIZE),
                    FILE_BLOCK_SIZE,
                )
                packed[block, place // 2, rows] = tile_value(tile)

            pl.when(live)(take)
            place = place + jnp.where(live, 1, 0)

    dkv_sum[...] = jnp.zeros_like(dkv_sum)

    triangle = lax.broadcasted_iota(jnp.int32, (FILE_BLOCK_SIZE, FILE_BLOCK_SIZE), 0) <= (
        lax.broadcasted_iota(jnp.int32, (FILE_BLOCK_SIZE, FILE_BLOCK_SIZE), 1)
    )
    allowed = jnp.concatenate([triangle] * GROUP, axis=1)
    head_columns = [
        slice(head * HEAD_DIMENSION, (head + 1) * HEAD_DIMENSION) for head in range(HALF_KV)
    ]
    value_columns = [
        slice(HALF_KV_WIDTH + head * HEAD_DIMENSION, HALF_KV_WIDTH + (head + 1) * HEAD_DIMENSION)
        for head in range(HALF_KV)
    ]

    for block in range(SIDES):
        for head in range(HALF_KV):
            for member in range(GROUP):
                rows = slice(member * FILE_BLOCK_SIZE, (member + 1) * FILE_BLOCK_SIZE)
                start = (head * GROUP + member) * HEAD_DIMENSION
                columns = slice(start, start + HEAD_DIMENSION)
                if block == 0:
                    wide = pl.ds(pl.multiple_of(lane + start, HEAD_DIMENSION), HEAD_DIMENSION)
                    q_stack[head, rows, :] = q_ref[micro, 0, :, wide]
                    upstream = g_ref[0, :, wide]
                else:
                    q_stack[head, rows, :] = received_ref[0, :, columns]
                    upstream = received_ref[1, :, columns]
                if with_arrived:
                    upstream = (
                        upstream.astype(jnp.float32)
                        + arrived_ref[block, :, columns].astype(jnp.float32)
                    ).astype(jnp.bfloat16)
                g_stack[head, rows, :] = upstream

        def products(chunk, head):
            score = lax.dot_general(
                packed[block, chunk, :, head_columns[head]],
                q_stack[head],
                NT,
                preferred_element_type=jnp.float32,
            )
            dprobs[head, chunk] = lax.dot_general(
                packed[block, chunk, :, value_columns[head]],
                g_stack[head],
                NT,
                preferred_element_type=jnp.float32,
            )
            return score

        def first(chunk, largest):
            found = []
            for head in range(HALF_KV):
                score = products(chunk, head)
                scores[head, chunk] = score
                found.append(jnp.maximum(largest[head], fold_rows(score, jnp.max)))
            return tuple(found)

        largest = []
        for head in range(HALF_KV):
            score = products(0, head)
            score = jnp.concatenate(
                [
                    jnp.where(allowed, score[:FILE_BLOCK_SIZE], negative_large),
                    score[FILE_BLOCK_SIZE:] + jnp.where(evens[block], 0.0, negative_large),
                ],
                axis=0,
            )
            scores[head, 0] = score
            largest.append(fold_rows(score, jnp.max))
        largest = lax.fori_loop(1, chunks[block], first, tuple(largest))
        row_max = [jnp.max(value, axis=0, keepdims=True) for value in largest]

        def second(chunk, sums):
            found = []
            for head in range(HALF_KV):
                weight = jnp.exp2((scores[head, chunk] - row_max[head]) * EXP2_SCALE)
                scores[head, chunk] = weight
                found.append(sums[2 * head] + fold_rows(weight, jnp.sum))
                found.append(sums[2 * head + 1] + fold_rows(weight * dprobs[head, chunk], jnp.sum))
            return tuple(found)

        nothing = jnp.zeros((8, STACK), jnp.float32)
        sums = lax.fori_loop(0, chunks[block], second, (nothing,) * (2 * HALF_KV))
        inverse = [1.0 / jnp.sum(sums[2 * h], axis=0, keepdims=True) for h in range(HALF_KV)]
        delta = [
            jnp.sum(sums[2 * h + 1], axis=0, keepdims=True) * inverse[h] for h in range(HALF_KV)
        ]

        def third(chunk, totals):
            found = []
            tile_pair = [listing[block, 2 * chunk], listing[block, 2 * chunk + 1]]
            for head in range(HALF_KV):
                prob = scores[head, chunk] * inverse[head]
                score_grad = (prob * (dprobs[head, chunk] - delta[head])).astype(jnp.bfloat16)
                key_part = lax.dot_general(
                    score_grad, q_stack[head], NN, preferred_element_type=jnp.float32
                )
                value_part = lax.dot_general(
                    prob.astype(jnp.bfloat16), g_stack[head], NN, preferred_element_type=jnp.float32
                )
                for place in range(2):
                    rows = slice(place * FILE_BLOCK_SIZE, (place + 1) * FILE_BLOCK_SIZE)
                    dkv_sum[tile_pair[place], :, head_columns[head]] += key_part[rows]
                    dkv_sum[tile_pair[place], :, value_columns[head]] += value_part[rows]
                found.append(
                    totals[head]
                    + lax.dot_general(
                        packed[block, chunk, :, head_columns[head]],
                        score_grad,
                        TN,
                        preferred_element_type=jnp.float32,
                    )
                )
            return tuple(found)

        empty = jnp.zeros((HEAD_DIMENSION, STACK), jnp.float32)
        dq_turned = lax.fori_loop(0, chunks[block], third, (empty,) * HALF_KV)
        for head in range(HALF_KV):
            for member in range(GROUP):
                start = (head * GROUP + member) * HEAD_DIMENSION
                part = dq_turned[head][:, member * FILE_BLOCK_SIZE : (member + 1) * FILE_BLOCK_SIZE]
                dq_ref[block, :, start : start + HEAD_DIMENSION] = (part.T * SCALE).astype(
                    jnp.bfloat16
                )

    for tile in range(tiles):
        out, chain = dkv_refs[tile // SIDES], tile % SIDES
        out[chain, :, :HALF_KV_WIDTH] = (dkv_sum[tile, :, :HALF_KV_WIDTH] * SCALE).astype(
            jnp.bfloat16
        )
        out[chain, :, HALF_KV_WIDTH:] = dkv_sum[tile, :, HALF_KV_WIDTH:].astype(jnp.bfloat16)


def backward(lines, micro, imports, block_ids, queries, gradient, received, arrived, kv_parts):
    tiles = lines * SIDES
    with_arrived = arrived is not None
    vmem = pl.BlockSpec(memory_space=pltpu.VMEM)
    smem = pl.BlockSpec(memory_space=pltpu.SMEM)
    operands = [imports, block_ids, queries, gradient, received]
    if with_arrived:
        operands.append(arrived)
    operands += kv_parts
    query_shape = (SIDES, FILE_BLOCK_SIZE, HALF_Q_WIDTH)
    key_shape = (SIDES, FILE_BLOCK_SIZE, 2 * HALF_KV_WIDTH)

    def body(*refs):
        backward_kernel(lines, micro, with_arrived, len(kv_parts), *refs)

    stacked = (HALF_KV, STACK, HEAD_DIMENSION)
    squares = (HALF_KV, tiles // 2, 2 * FILE_BLOCK_SIZE, STACK)
    scratch = [
        pltpu.VMEM((SIDES, tiles // 2, 2 * FILE_BLOCK_SIZE, 2 * HALF_KV_WIDTH), jnp.bfloat16),
        pltpu.VMEM(stacked, jnp.bfloat16),
        pltpu.VMEM(stacked, jnp.bfloat16),
        pltpu.VMEM(squares, jnp.float32),
        pltpu.VMEM(squares, jnp.float32),
        pltpu.VMEM((tiles, FILE_BLOCK_SIZE, 2 * HALF_KV_WIDTH), jnp.float32),
    ]
    needed = sum(math.prod(block.shape) * block.dtype.itemsize for block in scratch)
    needed += sum(math.prod(block.shape) * 2 for block in operands[2:])
    needed += math.prod(query_shape) * 2 + lines * math.prod(key_shape) * 2
    results = pl.pallas_call(
        body,
        out_shape=[jax.ShapeDtypeStruct(query_shape, jnp.bfloat16)]
        + [jax.ShapeDtypeStruct(key_shape, jnp.bfloat16)] * lines,
        in_specs=[smem, smem] + [vmem] * (len(operands) - 2),
        out_specs=[vmem] * (1 + lines),
        scratch_shapes=scratch + [pltpu.SMEM((SIDES, tiles), jnp.int32)],
        compiler_params=pltpu.CompilerParams(vmem_limit_bytes=needed + 6 * 1024 * 1024),
        cost_estimate=pl.CostEstimate(
            flops=10 * 10**9, bytes_accessed=4 * 10**6, transcendentals=0
        ),
    )(*operands)
    return results[0], results[1:]


def side_columns(of_side, width, start=0):
    return pl.ds(pl.multiple_of(start + of_side * width, HEAD_DIMENSION), width)


def my_side():
    return lax.rem(lax.axis_index("ctx"), SIDES)


def small_call(kernel, shapes, operands):
    vmem = pl.BlockSpec(memory_space=pltpu.VMEM)
    moved = sum(math.prod(block.shape) * 2 for block in operands)
    return pl.pallas_call(
        kernel,
        out_shape=[jax.ShapeDtypeStruct(shape, jnp.bfloat16) for shape in shapes],
        in_specs=[vmem] * len(operands),
        out_specs=[vmem] * len(shapes),
        compiler_params=pltpu.CompilerParams(vmem_limit_bytes=2 * moved + 4 * 1024 * 1024),
        cost_estimate=pl.CostEstimate(flops=0, bytes_accessed=2 * moved, transcendentals=0),
    )(*operands)


def split_keys_kernel(key_ref, value_ref, own_a_ref, own_b_ref, given_ref):
    side = my_side()
    own_refs = (own_a_ref, own_b_ref)
    for micro in range(MICRO_BATCHES):
        for place, ref in enumerate((key_ref, value_ref)):
            columns = slice(place * HALF_KV_WIDTH, (place + 1) * HALF_KV_WIDTH)
            own_refs[micro][:, columns] = ref[micro, 0, :, side_columns(side, HALF_KV_WIDTH)]
            given_ref[micro, :, columns] = ref[micro, 0, :, side_columns(1 - side, HALF_KV_WIDTH)]


def split_rows_kernel(micro, query_ref, gradient_ref, given_ref):
    columns = side_columns(1 - my_side(), HALF_Q_WIDTH)
    given_ref[0] = query_ref[micro, 0, :, columns]
    given_ref[1] = gradient_ref[0, :, columns]


def join_rows_kernel(own_ref, received_ref, out_ref):
    side = my_side()
    out_ref[0, :, side_columns(side, HALF_Q_WIDTH)] = own_ref[0]
    out_ref[0, :, side_columns(1 - side, HALF_Q_WIDTH)] = received_ref[...]


def assemble_kernel(sum_ref, crossed_ref, local_ref, *refs):
    *moved_refs, out_ref = refs
    half = len(moved_refs) // 2
    side = my_side()
    for micro in range(MICRO_BATCHES):
        if micro == 0:
            halves = (sum_ref[0], crossed_ref[...])
        else:
            halves = []
            for parts in (
                [local_ref[0]] + [ref[...] for ref in moved_refs[:half]],
                [ref[...] for ref in moved_refs[half:]],
            ):
                total = parts[0].astype(jnp.float32)
                for block in parts[1:]:
                    total = total + block.astype(jnp.float32)
                halves.append(total.astype(jnp.bfloat16))
        for total, of_side in zip(halves, (side, 1 - side)):
            for kind in range(2):
                start = kind * KEY_VALUE_HEADS * HEAD_DIMENSION
                out_ref[micro, 0, :, side_columns(of_side, HALF_KV_WIDTH, start)] = total[
                    :, kind * HALF_KV_WIDTH : (kind + 1) * HALF_KV_WIDTH
                ]


def on_device(queries, keys, values, grad_a, grad_b, imports, block_ids):
    devices = lax.axis_size("ctx")
    lines = devices // SIDES
    masks = line_masks(lines)
    offsets = line_offsets(lines)
    pipe = lax.axis_size("pipe")
    key_shape = (FILE_BLOCK_SIZE, 2 * HALF_KV_WIDTH)
    row_shape = (FILE_BLOCK_SIZE, HALF_Q_WIDTH)

    def moved(block, mask, crossing=0):
        route = [(i, i ^ (mask * SIDES + crossing)) for i in range(devices)]
        return lax.ppermute(block, "ctx", route)

    def swap(block):
        return moved(block, 0, 1)

    def down(block):
        return lax.ppermute(block, "pipe", [(i + 1, i) for i in range(pipe - 1)])

    def given_rows(micro, query_rows, gradient_rows):
        def kernel(*refs):
            split_rows_kernel(micro, *refs)

        return small_call(kernel, [(2,) + row_shape], [query_rows, gradient_rows])[0]

    def joined(own, received):
        shape = (1, FILE_BLOCK_SIZE, SIDES * HALF_Q_WIDTH)
        return small_call(join_rows_kernel, [shape], [own, received])[0]

    def together(*values):
        return list(lax.optimization_barrier(values))

    def add(*blocks):
        total = blocks[0].astype(jnp.float32)
        for block in blocks[1:]:
            total = total + block.astype(jnp.float32)
        return total.astype(jnp.bfloat16)

    def gathered(unit):
        units = [unit]
        for mask in masks:
            units += [moved(block, mask) for block in units]
        return units

    def nearer_sums(parts, last_waits=False):
        held = {offset: [part] for offset, part in zip(offsets, parts)}
        for level in range(len(masks) - 1, 0, -1):
            kept = offsets[: 1 << level]
            found = {}
            for offset in reversed(kept):
                near, far = add(*held[offset]), add(*held[offset ^ masks[level]])
                if offset == 0 and last_waits:
                    far = together(far, *found[masks[0]])[0]
                found[offset] = [near, moved(far, masks[level])]
            held = found
        return held

    own, own_b, given = small_call(
        split_keys_kernel, [key_shape, key_shape, (MICRO_BATCHES,) + key_shape], [keys, values]
    )
    others = swap(given)
    rows_a = swap(given_rows(0, queries, grad_a))
    tiles_a = []
    for pair in zip(gathered(own), gathered(others[0])):
        tiles_a += pair

    queries_b, gradient_b, _ = together(queries, grad_b, tiles_a[2])
    rows_b = swap(given_rows(1, queries_b, gradient_b))
    unit_b, rows_a, _ = together(jnp.stack([own_b, others[1]]), rows_a, tiles_a[3])
    early = [moved(unit_b, mask) for mask in masks]

    dq_a, dkv_a = backward(
        lines, 0, imports, block_ids, queries, grad_a, rows_a, None, tiles_a
    )
    dq_a, *rest = together(dq_a, *early, *dkv_a)
    early, dkv_a = rest[: len(masks)], rest[len(masks) :]
    arrived = down(dq_a)
    units_b = [unit_b]
    for mask, fresh in zip(masks, early):
        units_b += [fresh] + [moved(block, mask) for block in units_b[1:]]
    held_a = nearer_sums(dkv_a, True)
    far_a = add(*held_a[masks[0]])
    mirrored_a = moved(far_a, masks[0])
    near_a = held_a[0]
    back_a = swap(dq_a[1])
    dq_b, dkv_b = backward(
        lines, 1, imports, block_ids, queries, grad_b, rows_b, arrived, units_b
    )
    held_b = nearer_sums(dkv_b)
    near_b, back_a, mirrored_a, *near_a = together(
        held_b[masks[0]][-1], back_a, mirrored_a, *near_a
    )
    held_b[masks[0]][-1] = near_b
    far_b, local_b = add(*held_b[masks[0]]), add(*held_b[0])
    pieces_b = [
        local_b,
        moved(far_b[0], masks[0]),
        moved(far_b[1], masks[0], 1),
        swap(local_b[1]),
    ]
    sum_a = add(*near_a, mirrored_a)
    crossed_a = swap(sum_a[1])
    back_b = swap(dq_b[1])
    out_a = joined(dq_a, back_a)
    out_b = joined(dq_b, back_b)
    kv_shape = (MICRO_BATCHES, 1, FILE_BLOCK_SIZE, 2 * KEY_VALUE_HEADS * HEAD_DIMENSION)
    kv = small_call(assemble_kernel, [kv_shape], [sum_a, crossed_a, *pieces_b])[0]
    return out_a, out_b, kv


def solution(mesh):
    return jax.shard_map(
        on_device,
        mesh=mesh,
        in_specs=(
            P(None, "pipe", "ctx", None),
            P(None, "pipe", "ctx", None),
            P(None, "pipe", "ctx", None),
            P("pipe", "ctx", None),
            P("pipe", "ctx", None),
            P(None, "pipe", None, None),
            P(None, "pipe", None),
        ),
        out_specs=(P("pipe", "ctx", None), P("pipe", "ctx", None), P(None, "pipe", "ctx", None)),
        check_vma=False,
    )
```

```python
import math

import jax
import jax.numpy as jnp
from jax import lax
from jax.experimental import pallas as pl
from jax.experimental.pallas import tpu as pltpu
from jax.sharding import PartitionSpec as P

QUERY_HEADS = 20
KEY_VALUE_HEADS = 4
HEAD_DIMENSION = 128
FILE_BLOCK_SIZE = 128
MICRO_BATCHES = 2

GROUP = QUERY_HEADS // KEY_VALUE_HEADS
SIDES = 2
HALF_KV = KEY_VALUE_HEADS // SIDES
HALF_Q_WIDTH = HALF_KV * GROUP * HEAD_DIMENSION
HALF_KV_WIDTH = HALF_KV * HEAD_DIMENSION
STACK = GROUP * FILE_BLOCK_SIZE
negative_large = -1e30
SCALE = 1.0 / math.sqrt(HEAD_DIMENSION)
EXP2_SCALE = SCALE * math.log2(math.e)

NT = (((1,), (1,)), ((), ()))
NN = (((1,), (0,)), ((), ()))
TN = (((0,), (0,)), ((), ()))


def line_masks(lines):
    masks = []
    while lines > 1:
        masks.append(lines - 1)
        lines //= 2
    return masks


def line_offsets(lines):
    offsets = [0]
    for mask in line_masks(lines):
        offsets += [offset ^ mask for offset in offsets]
    return offsets


def fold_rows(tile, op):
    rows, columns = tile.shape
    return op(tile.reshape(rows // 8, 8, columns), axis=0)


def backward_kernel(lines, micro, with_arrived, kv_count, *refs):
    tiles = lines * SIDES
    refs = list(refs)
    imports_ref, ids_ref, q_ref, g_ref, received_ref = refs[:5]
    at = 5
    arrived_ref = None
    if with_arrived:
        arrived_ref = refs[at]
        at += 1
    kv_refs = refs[at : at + kv_count]
    at += kv_count
    dq_ref = refs[at]
    at += 1
    dkv_refs = refs[at : at + lines]
    at += lines
    packed, q_stack, g_stack, scores, dprobs, dkv_sum, dq_sum, listing = refs[at:]

    me = lax.axis_index("ctx")
    line, side = me // SIDES, lax.rem(me, SIDES)
    offsets = line_offsets(lines)
    lane = side * HALF_Q_WIDTH

    def tile_value(tile):
        if kv_count == tiles:
            return kv_refs[tile][...]
        return kv_refs[tile // SIDES][tile % SIDES]

    evens, chunks = [], []
    for block in range(SIDES):
        query_slot = line * SIDES + (side if block == 0 else 1 - side)
        query_id = ids_ref[micro, 0, query_slot]
        others = []
        total = jnp.int32(1)
        for tile in range(tiles):
            if tile == block:
                continue
            step, chain = tile // SIDES, tile % SIDES
            key_line = jnp.bitwise_xor(line, offsets[step])
            key_slot = key_line * SIDES + (side if chain == 0 else 1 - side)
            key_id = ids_ref[micro, 0, key_slot]
            live = imports_ref[micro, 0, query_id, key_id] > 0
            others.append((tile, live))
            total = total + jnp.where(live, 1, 0)
        even = lax.rem(total, 2) == 0
        evens.append(even)
        chunks.append((total + 1) // 2)
        listing[block, 0] = block
        listing[block, 1] = block
        packed[block, 0, :FILE_BLOCK_SIZE] = tile_value(block)
        packed[block, 0, FILE_BLOCK_SIZE:] = tile_value(block)
        place = jnp.where(even, 1, 2)
        for tile, live in others:

            def take(block=block, place=place, tile=tile):
                listing[block, place] = tile
                rows = pl.ds(
                    pl.multiple_of(lax.rem(place, 2) * FILE_BLOCK_SIZE, FILE_BLOCK_SIZE),
                    FILE_BLOCK_SIZE,
                )
                packed[block, place // 2, rows] = tile_value(tile)

            pl.when(live)(take)
            place = place + jnp.where(live, 1, 0)

    dkv_sum[...] = jnp.zeros_like(dkv_sum)

    triangle = lax.broadcasted_iota(jnp.int32, (FILE_BLOCK_SIZE, FILE_BLOCK_SIZE), 0) <= (
        lax.broadcasted_iota(jnp.int32, (FILE_BLOCK_SIZE, FILE_BLOCK_SIZE), 1)
    )
    allowed = jnp.concatenate([triangle] * GROUP, axis=1)
    head_columns = [
        slice(head * HEAD_DIMENSION, (head + 1) * HEAD_DIMENSION) for head in range(HALF_KV)
    ]
    value_columns = [
        slice(HALF_KV_WIDTH + head * HEAD_DIMENSION, HALF_KV_WIDTH + (head + 1) * HEAD_DIMENSION)
        for head in range(HALF_KV)
    ]

    for block in range(SIDES):
        for head in range(HALF_KV):
            for member in range(GROUP):
                rows = slice(member * FILE_BLOCK_SIZE, (member + 1) * FILE_BLOCK_SIZE)
                start = (head * GROUP + member) * HEAD_DIMENSION
                columns = slice(start, start + HEAD_DIMENSION)
                if block == 0:
                    wide = pl.ds(pl.multiple_of(lane + start, HEAD_DIMENSION), HEAD_DIMENSION)
                    q_stack[head, rows, :] = q_ref[micro, 0, :, wide]
                    upstream = g_ref[0, :, wide]
                else:
                    q_stack[head, rows, :] = received_ref[0, :, columns]
                    upstream = received_ref[1, :, columns]
                if with_arrived:
                    upstream = (
                        upstream.astype(jnp.float32)
                        + arrived_ref[block, :, columns].astype(jnp.float32)
                    ).astype(jnp.bfloat16)
                g_stack[head, rows, :] = upstream

        def products(chunk, head):
            score = lax.dot_general(
                packed[block, chunk, :, head_columns[head]],
                q_stack[head],
                NT,
                preferred_element_type=jnp.float32,
            )
            dprobs[head, chunk] = lax.dot_general(
                packed[block, chunk, :, value_columns[head]],
                g_stack[head],
                NT,
                preferred_element_type=jnp.float32,
            )
            return score

        def first(chunk, largest):
            found = []
            for head in range(HALF_KV):
                score = products(chunk, head)
                scores[head, chunk] = score
                found.append(jnp.maximum(largest[head], fold_rows(score, jnp.max)))
            return tuple(found)

        largest = []
        for head in range(HALF_KV):
            score = products(0, head)
            score = jnp.concatenate(
                [
                    jnp.where(allowed, score[:FILE_BLOCK_SIZE], negative_large),
                    score[FILE_BLOCK_SIZE:] + jnp.where(evens[block], 0.0, negative_large),
                ],
                axis=0,
            )
            scores[head, 0] = score
            largest.append(fold_rows(score, jnp.max))
        largest = lax.fori_loop(1, chunks[block], first, tuple(largest))
        row_max = [jnp.max(value, axis=0, keepdims=True) for value in largest]

        def second(chunk, sums):
            found = []
            for head in range(HALF_KV):
                weight = jnp.exp2((scores[head, chunk] - row_max[head]) * EXP2_SCALE)
                scores[head, chunk] = weight
                found.append(sums[2 * head] + fold_rows(weight, jnp.sum))
                found.append(sums[2 * head + 1] + fold_rows(weight * dprobs[head, chunk], jnp.sum))
            return tuple(found)

        nothing = jnp.zeros((8, STACK), jnp.float32)
        sums = lax.fori_loop(0, chunks[block], second, (nothing,) * (2 * HALF_KV))
        inverse = [1.0 / jnp.sum(sums[2 * h], axis=0, keepdims=True) for h in range(HALF_KV)]
        delta = [
            jnp.sum(sums[2 * h + 1], axis=0, keepdims=True) * inverse[h] for h in range(HALF_KV)
        ]

        def third(chunk, carried):
            tile_pair = [listing[block, 2 * chunk], listing[block, 2 * chunk + 1]]
            for head in range(HALF_KV):
                prob = scores[head, chunk] * inverse[head]
                score_grad = (prob * (dprobs[head, chunk] - delta[head])).astype(jnp.bfloat16)
                key_part = lax.dot_general(
                    score_grad, q_stack[head], NN, preferred_element_type=jnp.float32
                )
                value_part = lax.dot_general(
                    prob.astype(jnp.bfloat16), g_stack[head], NN, preferred_element_type=jnp.float32
                )
                for place in range(2):
                    rows = slice(place * FILE_BLOCK_SIZE, (place + 1) * FILE_BLOCK_SIZE)
                    dkv_sum[tile_pair[place], :, head_columns[head]] += key_part[rows]
                    dkv_sum[tile_pair[place], :, value_columns[head]] += value_part[rows]
                dq_sum[head] += lax.dot_general(
                    packed[block, chunk, :, head_columns[head]],
                    score_grad,
                    TN,
                    preferred_element_type=jnp.float32,
                )
            return carried

        dq_sum[...] = jnp.zeros_like(dq_sum)
        lax.fori_loop(0, chunks[block], third, 0)
        dq_turned = [dq_sum[head] for head in range(HALF_KV)]
        for head in range(HALF_KV):
            for member in range(GROUP):
                start = (head * GROUP + member) * HEAD_DIMENSION
                part = dq_turned[head][:, member * FILE_BLOCK_SIZE : (member + 1) * FILE_BLOCK_SIZE]
                dq_ref[block, :, start : start + HEAD_DIMENSION] = (part.T * SCALE).astype(
                    jnp.bfloat16
                )

    for tile in range(tiles):
        out, chain = dkv_refs[tile // SIDES], tile % SIDES
        out[chain, :, :HALF_KV_WIDTH] = (dkv_sum[tile, :, :HALF_KV_WIDTH] * SCALE).astype(
            jnp.bfloat16
        )
        out[chain, :, HALF_KV_WIDTH:] = dkv_sum[tile, :, HALF_KV_WIDTH:].astype(jnp.bfloat16)


def backward(lines, micro, imports, block_ids, queries, gradient, received, arrived, kv_parts):
    tiles = lines * SIDES
    with_arrived = arrived is not None
    vmem = pl.BlockSpec(memory_space=pltpu.VMEM)
    smem = pl.BlockSpec(memory_space=pltpu.SMEM)
    operands = [imports, block_ids, queries, gradient, received]
    if with_arrived:
        operands.append(arrived)
    operands += kv_parts
    query_shape = (SIDES, FILE_BLOCK_SIZE, HALF_Q_WIDTH)
    key_shape = (SIDES, FILE_BLOCK_SIZE, 2 * HALF_KV_WIDTH)

    def body(*refs):
        backward_kernel(lines, micro, with_arrived, len(kv_parts), *refs)

    stacked = (HALF_KV, STACK, HEAD_DIMENSION)
    squares = (HALF_KV, tiles // 2, 2 * FILE_BLOCK_SIZE, STACK)
    scratch = [
        pltpu.VMEM((SIDES, tiles // 2, 2 * FILE_BLOCK_SIZE, 2 * HALF_KV_WIDTH), jnp.bfloat16),
        pltpu.VMEM(stacked, jnp.bfloat16),
        pltpu.VMEM(stacked, jnp.bfloat16),
        pltpu.VMEM(squares, jnp.float32),
        pltpu.VMEM(squares, jnp.float32),
        pltpu.VMEM((tiles, FILE_BLOCK_SIZE, 2 * HALF_KV_WIDTH), jnp.float32),
        pltpu.VMEM((HALF_KV, HEAD_DIMENSION, STACK), jnp.float32),
    ]
    needed = sum(math.prod(block.shape) * block.dtype.itemsize for block in scratch)
    needed += sum(math.prod(block.shape) * 2 for block in operands[2:])
    needed += math.prod(query_shape) * 2 + lines * math.prod(key_shape) * 2
    results = pl.pallas_call(
        body,
        out_shape=[jax.ShapeDtypeStruct(query_shape, jnp.bfloat16)]
        + [jax.ShapeDtypeStruct(key_shape, jnp.bfloat16)] * lines,
        in_specs=[smem, smem] + [vmem] * (len(operands) - 2),
        out_specs=[vmem] * (1 + lines),
        scratch_shapes=scratch + [pltpu.SMEM((SIDES, tiles), jnp.int32)],
        compiler_params=pltpu.CompilerParams(vmem_limit_bytes=needed + 6 * 1024 * 1024),
        cost_estimate=pl.CostEstimate(
            flops=10 * 10**9, bytes_accessed=4 * 10**6, transcendentals=0
        ),
    )(*operands)
    return results[0], results[1:]


def side_columns(of_side, width, start=0):
    return pl.ds(pl.multiple_of(start + of_side * width, HEAD_DIMENSION), width)


def my_side():
    return lax.rem(lax.axis_index("ctx"), SIDES)


def small_call(kernel, shapes, operands):
    vmem = pl.BlockSpec(memory_space=pltpu.VMEM)
    moved = sum(math.prod(block.shape) * 2 for block in operands)
    return pl.pallas_call(
        kernel,
        out_shape=[jax.ShapeDtypeStruct(shape, jnp.bfloat16) for shape in shapes],
        in_specs=[vmem] * len(operands),
        out_specs=[vmem] * len(shapes),
        compiler_params=pltpu.CompilerParams(vmem_limit_bytes=2 * moved + 4 * 1024 * 1024),
        cost_estimate=pl.CostEstimate(flops=0, bytes_accessed=2 * moved, transcendentals=0),
    )(*operands)


def split_keys_kernel(key_ref, value_ref, own_a_ref, own_b_ref, given_ref):
    side = my_side()
    own_refs = (own_a_ref, own_b_ref)
    for micro in range(MICRO_BATCHES):
        for place, ref in enumerate((key_ref, value_ref)):
            columns = slice(place * HALF_KV_WIDTH, (place + 1) * HALF_KV_WIDTH)
            own_refs[micro][:, columns] = ref[micro, 0, :, side_columns(side, HALF_KV_WIDTH)]
            given_ref[micro, :, columns] = ref[micro, 0, :, side_columns(1 - side, HALF_KV_WIDTH)]


def split_rows_kernel(micro, query_ref, gradient_ref, given_ref):
    columns = side_columns(1 - my_side(), HALF_Q_WIDTH)
    given_ref[0] = query_ref[micro, 0, :, columns]
    given_ref[1] = gradient_ref[0, :, columns]


def join_rows_kernel(own_ref, received_ref, out_ref):
    side = my_side()
    out_ref[0, :, side_columns(side, HALF_Q_WIDTH)] = own_ref[0]
    out_ref[0, :, side_columns(1 - side, HALF_Q_WIDTH)] = received_ref[...]


def assemble_kernel(sum_ref, crossed_ref, local_ref, *refs):
    *moved_refs, out_ref = refs
    half = len(moved_refs) // 2
    side = my_side()
    for micro in range(MICRO_BATCHES):
        if micro == 0:
            halves = (sum_ref[0], crossed_ref[...])
        else:
            halves = []
            for parts in (
                [local_ref[0]] + [ref[...] for ref in moved_refs[:half]],
                [ref[...] for ref in moved_refs[half:]],
            ):
                total = parts[0].astype(jnp.float32)
                for block in parts[1:]:
                    total = total + block.astype(jnp.float32)
                halves.append(total.astype(jnp.bfloat16))
        for total, of_side in zip(halves, (side, 1 - side)):
            for kind in range(2):
                start = kind * KEY_VALUE_HEADS * HEAD_DIMENSION
                out_ref[micro, 0, :, side_columns(of_side, HALF_KV_WIDTH, start)] = total[
                    :, kind * HALF_KV_WIDTH : (kind + 1) * HALF_KV_WIDTH
                ]


def on_device(queries, keys, values, grad_a, grad_b, imports, block_ids):
    devices = lax.axis_size("ctx")
    lines = devices // SIDES
    masks = line_masks(lines)
    offsets = line_offsets(lines)
    pipe = lax.axis_size("pipe")
    key_shape = (FILE_BLOCK_SIZE, 2 * HALF_KV_WIDTH)
    row_shape = (FILE_BLOCK_SIZE, HALF_Q_WIDTH)

    def moved(block, mask, crossing=0):
        route = [(i, i ^ (mask * SIDES + crossing)) for i in range(devices)]
        return lax.ppermute(block, "ctx", route)

    def swap(block):
        return moved(block, 0, 1)

    def down(block):
        return lax.ppermute(block, "pipe", [(i + 1, i) for i in range(pipe - 1)])

    def given_rows(micro, query_rows, gradient_rows):
        def kernel(*refs):
            split_rows_kernel(micro, *refs)

        return small_call(kernel, [(2,) + row_shape], [query_rows, gradient_rows])[0]

    def joined(own, received):
        shape = (1, FILE_BLOCK_SIZE, SIDES * HALF_Q_WIDTH)
        return small_call(join_rows_kernel, [shape], [own, received])[0]

    def together(*values):
        return list(lax.optimization_barrier(values))

    def add(*blocks):
        total = blocks[0].astype(jnp.float32)
        for block in blocks[1:]:
            total = total + block.astype(jnp.float32)
        return total.astype(jnp.bfloat16)

    def gathered(unit):
        units = [unit]
        for mask in masks:
            units += [moved(block, mask) for block in units]
        return units

    def nearer_sums(parts, last_waits=False):
        held = {offset: [part] for offset, part in zip(offsets, parts)}
        for level in range(len(masks) - 1, 0, -1):
            kept = offsets[: 1 << level]
            found = {}
            for offset in reversed(kept):
                near, far = add(*held[offset]), add(*held[offset ^ masks[level]])
                if offset == 0 and last_waits:
                    far = together(far, *found[masks[0]])[0]
                found[offset] = [near, moved(far, masks[level])]
            held = found
        return held

    own, own_b, given = small_call(
        split_keys_kernel, [key_shape, key_shape, (MICRO_BATCHES,) + key_shape], [keys, values]
    )
    others = swap(given)
    rows_a = swap(given_rows(0, queries, grad_a))
    tiles_a = []
    for pair in zip(gathered(own), gathered(others[0])):
        tiles_a += pair

    queries_b, gradient_b, _ = together(queries, grad_b, tiles_a[3])
    rows_b = swap(given_rows(1, queries_b, gradient_b))
    unit_b, rows_a, _ = together(jnp.stack([own_b, others[1]]), rows_a, tiles_a[4])
    early = [moved(unit_b, mask) for mask in masks]

    dq_a, dkv_a = backward(
        lines, 0, imports, block_ids, queries, grad_a, rows_a, None, tiles_a
    )
    dq_a, *rest = together(dq_a, *early, *dkv_a)
    early, dkv_a = rest[: len(masks)], rest[len(masks) :]
    arrived = down(dq_a)
    units_b = [unit_b]
    for mask, fresh in zip(masks, early):
        units_b += [fresh] + [moved(block, mask) for block in units_b[1:]]
    held_a = nearer_sums(dkv_a)
    far_a = add(*held_a[masks[0]])
    mirrored_a = moved(far_a, masks[0])
    near_a = held_a[0]
    back_a = swap(dq_a[1])
    dq_b, dkv_b = backward(
        lines, 1, imports, block_ids, queries, grad_b, rows_b, arrived, units_b
    )
    held_b = nearer_sums(dkv_b)
    near_b, back_a, mirrored_a, *near_a = together(
        held_b[masks[0]][-1], back_a, mirrored_a, *near_a
    )
    held_b[masks[0]][-1] = near_b
    far_b, local_b = add(*held_b[masks[0]]), add(*held_b[0])
    pieces_b = [
        local_b,
        moved(far_b[0], masks[0]),
        moved(far_b[1], masks[0], 1),
        swap(local_b[1]),
    ]
    sum_a = add(*near_a, mirrored_a)
    crossed_a = swap(sum_a[1])
    back_b = swap(dq_b[1])
    out_a = joined(dq_a, back_a)
    out_b = joined(dq_b, back_b)
    kv_shape = (MICRO_BATCHES, 1, FILE_BLOCK_SIZE, 2 * KEY_VALUE_HEADS * HEAD_DIMENSION)
    kv = small_call(assemble_kernel, [kv_shape], [sum_a, crossed_a, *pieces_b])[0]
    return out_a, out_b, kv


def solution(mesh):
    return jax.shard_map(
        on_device,
        mesh=mesh,
        in_specs=(
            P(None, "pipe", "ctx", None),
            P(None, "pipe", "ctx", None),
            P(None, "pipe", "ctx", None),
            P("pipe", "ctx", None),
            P("pipe", "ctx", None),
            P(None, "pipe", None, None),
            P(None, "pipe", None),
        ),
        out_specs=(P("pipe", "ctx", None), P("pipe", "ctx", None), P(None, "pipe", "ctx", None)),
        check_vma=False,
    )
```
